32 devices in a mesh: groups: 2 (over x), heads: 16 (over z, y, core).
Axes of the slice: x: 2, y: 2, z: 4, core: 2. Of those that a mesh axis runs over, the one named last changes fastest.
Arguments:
- prompt_hidden: bfloat16 [8192, 7168], P(('groups', 'heads')), parts along dimension 0, may hold values from -6 to 6
- prompt_len: int32 [4], P('groups'), parts along dimension 0, may hold values from 1 to 2048, 2560 in all
- owners: int32 [4], P('groups'), parts along dimension 0, may hold values from 0 to 15
- down_weight: bfloat16 [7168, 576], P('heads'), may hold values from -0.0625 to 0.0625
- latent_gain: float32 [512], replicated, may hold values from 0.5 to 1.5
- decode_hidden: bfloat16 [16, 7168], P('groups'), parts along dimension 0, may hold values from -6 to 6
- context_len: int32 [16], P('groups'), parts along dimension 0, may hold values from 256 to 1024, as said below
- query_nope: bfloat16 [16, 16, 128], P('groups', 'heads'), parts along dimension 0, may hold values from -6 to 6
- query_rope: bfloat16 [16, 16, 64], P('groups', 'heads'), parts along dimension 0, may hold values from -8 to 8
- key_absorb: bfloat16 [16, 128, 512], P('heads'), may hold values from -0.5 to 0.5
- value_absorb: bfloat16 [16, 512, 128], P('heads'), may hold values from -0.25 to 0.25
- out_weight: bfloat16 [2048, 7168], P('heads'), may hold values from -0.1875 to 0.1875
- cache: bfloat16 [16, 1024, 576], P('groups', 'heads'), parts along dimension 0, may hold values from -8 to 8
Outputs:
- new_cache: bfloat16 [4, 2048, 576], P('groups', 'heads'), parts along dimension 0
- attn_out: bfloat16 [16, 7168], P('groups'), parts along dimension 0
The draws below stay inside these ranges and needn't reach their ends.
There are 2 independent parts, one for each index of `groups`. The reference program is written for one: setup_inputs(seed, part) draws one part's arguments, and reference() takes and returns one part's arrays. A program takes and returns all parts, laid end to end along the dimension named above; an argument that names none is the same for every part. Nothing has to cross between parts.
Inputs may be any that keep to these rules, and one draw needn't show every extreme that they name: `prompt_len`: within each part (each index of groups) they sum to 2560. `context_len`: within each part some request has exactly 1024.
All inputs are finite; a program needn't handle non-finite values.
Results may differ from the reference program's by a relative error of at most 0.008.
Values may be sent and summed in bfloat16 or wider, within the bound.
A program may use at most 64 MiB of HBM per device.

```python
import math
import jax
import jax.numpy as jnp
import numpy as np
from jax import lax

D = 7168
LAT = 512
ROPE = 64
NOPE = 128
VDIM = 128
PMAX = 2048
DEC = 8
CROW_DEV = 64
HEADS = 16
NEWREQ = 2
CTX = 1024
N_HEADS = 16


def draw_query_rope(key, part):
    key = jax.random.fold_in(key, 1)
    drawn = jnp.clip(jax.random.normal(key, (DEC, HEADS, ROPE), jnp.float32), -6.0, 6.0)
    return drawn.astype(jnp.bfloat16)


def draw_cache(key, part):
    key = jax.random.fold_in(key, 2)
    drawn = jnp.clip(jax.random.normal(key, (DEC, CTX, LAT + ROPE), jnp.float32), -6.0, 6.0)
    return drawn.astype(jnp.bfloat16)


def draw_context_len(key, part):
    key = jax.random.fold_in(key, 3)
    lengths = jax.random.randint(key, (DEC,), CTX // 4, CTX + 1, dtype=jnp.int32)
    picked = jax.random.randint(jax.random.fold_in(key, 7), (), 0, DEC, dtype=jnp.int32)
    return jnp.where(jnp.arange(DEC, dtype=jnp.int32) == picked, jnp.int32(CTX), lengths).astype(jnp.int32)


def spiked(array, key, source, target, shards_of, factor):
    owner, partner = [(jnp.arange(array.shape[dim]) // (array.shape[dim] // shards_of)).reshape([-1 if axis == dim else 1 for axis in range(array.ndim)]) for dim in (source, target)]
    chosen = jax.random.permutation(key, shards_of)[partner]
    strong = (owner == chosen) | (owner == (partner + shards_of // 2) % shards_of)
    return jnp.where(strong, factor * array, array)


def block_levels(rng, dims, cuts, smallest, largest):
    def one(dim, parts):
        draws = jax.random.uniform(jax.random.fold_in(jax.random.fold_in(rng, 6), dim), (parts,), jnp.float32, smallest / len(cuts), largest / len(cuts))
        return jnp.repeat(jnp.exp(draws), dims[dim] // parts).reshape((-1,) + (1,) * (len(dims) - dim - 1))

    gain = one(*cuts[0])
    for cut in cuts[1:]:
        gain = gain * one(*cut)
    return gain


def profile(count, total, bound, lean):
    loads = [(1 << 20) // math.isqrt(rank ** lean) + 1 for rank in range(2, count + 1)]
    rest, holding = total - bound - (count - 1), [1] * (count - 1)
    while rest > 0:
        free = [i for i in range(count - 1) if holding[i] < bound]
        pool, left = sum([loads[i] for i in free]), rest
        for i in free:
            addition = min(bound - holding[i], max(1, left * loads[i] // pool), rest)
            holding[i] = holding[i] + addition
            rest = rest - addition
    return np.array([bound] + holding)


def uneven(rng, count, total, most, lean):
    if count == 2:
        one = jax.random.randint(rng, (), max(1, total - most), min(most, total - 1) + 1)
        return jnp.stack([one, total - one])
    tallies = jnp.asarray(profile(count, total, most, lean), jnp.int32)
    twos = (count - 1) // 2
    source_of, taker = tallies[1:1 + 2 * twos:2], tallies[2:2 + 2 * twos:2]
    room = jnp.minimum(source_of - 1, most - taker)
    moved = jax.random.randint(jax.random.fold_in(rng, 1), (twos,), 0, 1 << 20) % (room + 1)
    tallies = tallies.at[1:1 + 2 * twos:2].set(source_of - moved).at[2:2 + 2 * twos:2].set(taker + moved)
    return tallies[jax.random.permutation(jax.random.fold_in(rng, 2), count)]


def normal_values(stream_key, dims, scale, limit, cuts=(), kind=jnp.bfloat16):
    loudness = block_levels(stream_key, dims, cuts, -0.22, 0.18) if cuts else 1.0
    values = jax.random.normal(stream_key, dims, jnp.float32) * scale * loudness
    return jnp.minimum(jnp.maximum(values, -limit), limit).astype(kind)


def gaussian_with(key, shape, spread, most, pieces, heavy, kind=jnp.bfloat16):
    array = spread * jax.random.normal(key, shape, jnp.float32)
    if pieces:
        array = array * block_levels(key, shape, pieces, -0.22, 0.18)
    return jnp.clip(spiked(array, jax.random.fold_in(key, 3), *heavy), -most, most).astype(kind)


def setup_inputs(seed: int = 0, part: int = 0) -> dict:
    key_list = jax.random.split(jax.random.key(seed), 14)
    part_splits = jax.random.split(jax.random.fold_in(key_list[13], part), 14)
    prompt_hidden = normal_values(part_splits[0], (NEWREQ * PMAX, D), 1.0, 6.0, ((0, 16),))
    prompt_len = uneven(part_splits[1], NEWREQ, 5 * NEWREQ * PMAX // 8, PMAX, 2).astype(jnp.int32)
    owners = jax.random.randint(part_splits[2], (NEWREQ,), 0, N_HEADS).astype(jnp.int32)
    down_weight = normal_values(key_list[3], (D, LAT + ROPE), D ** -0.5, 0.0625, ((0, 16),))
    latent_gain = jnp.clip(1.0 + 0.1 * jax.random.normal(key_list[4], (LAT,), jnp.float32), 0.5, 1.5)
    decode_hidden = normal_values(part_splits[5], (DEC, D), 1.0, 6.0)
    context_len = draw_context_len(jax.random.fold_in(jax.random.fold_in(key_list[13], part), 71), part)
    query_nope = normal_values(part_splits[7], (DEC, HEADS, NOPE), 1.0, 6.0, ((1, 16),))
    query_rope = draw_query_rope(jax.random.fold_in(jax.random.fold_in(key_list[13], part), 71), part)
    key_absorb = normal_values(key_list[9], (HEADS, NOPE, LAT), NOPE ** -0.5, 0.5, ((0, 16),))
    value_absorb = normal_values(key_list[10], (HEADS, LAT, VDIM), LAT ** -0.5, 0.25, ((0, 16),))
    out_weight = gaussian_with(key_list[11], (HEADS * VDIM, D), (HEADS * VDIM) ** -0.5, 0.1875, ((0, 16),), (0, 1, 16, 2.0))
    cache = draw_cache(jax.random.fold_in(jax.random.fold_in(key_list[13], part), 71), part)
    return dict(prompt_hidden=prompt_hidden, prompt_len=prompt_len, owners=owners, down_weight=down_weight, latent_gain=latent_gain, decode_hidden=decode_hidden, context_len=context_len, query_nope=query_nope, query_rope=query_rope, key_absorb=key_absorb, value_absorb=value_absorb, out_weight=out_weight, cache=cache)


def latent_rows(kv_rows, positions, gain_vec):
    row_width = gain_vec.shape[0]
    latent = kv_rows[..., :row_width]
    rotary = kv_rows[..., row_width:]
    latent = latent * lax.rsqrt(lax.optimization_barrier(jnp.mean(latent * latent, axis=-1, keepdims=True)) + 1e-06) * gain_vec
    half_rope = rotary.shape[-1] // 2
    frequency = jnp.exp(jnp.arange(half_rope, dtype=jnp.float32) * (-math.log(10000.0) / half_rope))
    angles = positions.astype(jnp.float32)[..., None] * frequency
    cosine = jnp.cos(angles)
    sine_part = jnp.sin(angles)
    leading = rotary[..., :half_rope]
    second = rotary[..., half_rope:]
    turned = jnp.concatenate([leading * cosine - second * sine_part, second * cosine + leading * sine_part], axis=-1)
    return jnp.concatenate([latent, turned], axis=-1)

def reference(prompt_hidden, prompt_len, owners, down_weight, latent_gain, decode_hidden, context_len, query_nope, query_rope, key_absorb, value_absorb, out_weight, cache):
    row_width = LAT + ROPE
    positions = jnp.arange(PMAX, dtype=jnp.int32)
    rows_each = PMAX // N_HEADS

    def prefill_one(inputs):
        hidden, length, owner = inputs
        kv_rows = jnp.dot(hidden, down_weight, preferred_element_type=jnp.float32)
        entries = latent_rows(kv_rows, positions, latent_gain)
        entries = jnp.where((positions < length)[:, None], entries, jnp.float32(0.0)).astype(jnp.bfloat16)
        layout = entries.reshape(rows_each, N_HEADS, row_width)
        source = ((jnp.arange(N_HEADS, dtype=jnp.int32) - owner) % N_HEADS).astype(jnp.int32)
        rotated = jnp.take(layout, source, axis=1)
        return rotated.transpose(1, 0, 2).reshape(PMAX, row_width)
    new_cache = lax.map(prefill_one, (prompt_hidden.reshape(NEWREQ, PMAX, D), prompt_len, owners))
    kv_dec = jnp.dot(decode_hidden, down_weight, preferred_element_type=jnp.float32)
    own_keys = latent_rows(kv_dec, context_len, latent_gain).astype(jnp.bfloat16)
    query_latent = jnp.einsum('rhn,hnl->rhl', query_nope.astype(jnp.float32), key_absorb.astype(jnp.float32)).astype(jnp.bfloat16)
    query_abs = jnp.concatenate([query_latent, query_rope], axis=-1)
    score_scale = 1.0 / math.sqrt(NOPE + ROPE)
    slot_index = jnp.arange(CTX, dtype=jnp.int32)
    position = slot_index % CROW_DEV * N_HEADS + slot_index // CROW_DEV

    def decode_one(inputs):
        query, key_rows, length, own_key = inputs
        scores = jnp.dot(query, key_rows.T, preferred_element_type=jnp.float32) * score_scale
        is_live = position < length
        scores = jnp.where(is_live[None, :], scores, jnp.float32(-1e+30)).reshape(HEADS, N_HEADS, CROW_DEV)
        live_blocks = is_live.reshape(N_HEADS, CROW_DEV)
        block_max = lax.optimization_barrier(jnp.max(scores, axis=-1))
        weights = jnp.where(live_blocks[None], jnp.exp(scores - block_max[..., None]), jnp.float32(0.0))
        block_total = lax.optimization_barrier(jnp.sum(weights, axis=-1))
        values = key_rows[:, :LAT].reshape(N_HEADS, CROW_DEV, LAT)
        block_part = jnp.einsum('hbi,bil->hbl', weights.astype(jnp.bfloat16).astype(jnp.float32), values.astype(jnp.float32))
        own_score = jnp.dot(query, own_key, preferred_element_type=jnp.float32) * score_scale
        ceiling = jnp.maximum(lax.optimization_barrier(jnp.max(block_max, axis=-1)), own_score)
        factor = jnp.exp(block_max - ceiling[:, None])
        own_weight = jnp.exp(own_score - ceiling)
        summed = lax.optimization_barrier(jnp.sum(factor * block_total, axis=-1)) + own_weight
        gathered = lax.optimization_barrier(jnp.sum(factor[..., None] * block_part, axis=1)) + own_weight[:, None] * own_key[:LAT].astype(jnp.float32)[None, :]
        return (gathered / summed[:, None]).astype(jnp.bfloat16)
    latent_out = lax.map(decode_one, (query_abs, cache, context_len, own_keys))
    head_out = jnp.einsum('rhl,hlv->rhv', latent_out.astype(jnp.float32), value_absorb.astype(jnp.float32)).astype(jnp.bfloat16)
    attn_out = jnp.dot(head_out.reshape(DEC, HEADS * VDIM), out_weight, preferred_element_type=jnp.float32).astype(jnp.bfloat16)
    return (new_cache, attn_out)
```

```python
import math

import jax
import jax.numpy as jnp
from jax import lax
from jax.experimental import pallas as pl
from jax.experimental.pallas import tpu as pltpu
from jax.sharding import PartitionSpec as P

PSPLIT = 8


def latent_rows(kv_rows, positions, gain_vec):
    row_width = gain_vec.shape[0]
    latent = kv_rows[..., :row_width]
    rotary = kv_rows[..., row_width:]
    latent = (
        latent * lax.rsqrt(jnp.mean(latent * latent, axis=-1, keepdims=True) + 1e-06) * gain_vec
    )
    half_rope = rotary.shape[-1] // 2
    frequency = jnp.exp(jnp.arange(half_rope, dtype=jnp.float32) * (-math.log(10000.0) / half_rope))
    angles = positions.astype(jnp.float32)[..., None] * frequency
    cosine = jnp.cos(angles)
    sine_part = jnp.sin(angles)
    leading = rotary[..., :half_rope]
    second = rotary[..., half_rope:]
    turned = jnp.concatenate(
        [leading * cosine - second * sine_part, second * cosine + leading * sine_part], axis=-1
    )
    return jnp.concatenate([latent, turned], axis=-1)


def local(
    prompt_hidden,
    prompt_len,
    owners,
    down_weight,
    latent_gain,
    decode_hidden,
    context_len,
    query_nope,
    query_rope,
    key_absorb,
    value_absorb,
    out_weight,
    cache,
):
    members = lax.axis_size("heads")
    device = lax.axis_index("heads")
    rows_here, model_width = prompt_hidden.shape
    row_width = down_weight.shape[1]
    lat_width = latent_gain.shape[0]
    shard_rows = lax.all_gather(down_weight, "heads", axis=0, tiled=True)
    kv_new = jnp.dot(prompt_hidden, shard_rows, preferred_element_type=jnp.float32)
    kv_dec = jnp.dot(decode_hidden, shard_rows, preferred_element_type=jnp.float32)
    prompt_slot = device // PSPLIT
    length_here = lax.dynamic_index_in_dim(prompt_len, prompt_slot, 0, keepdims=False)
    owner_here = lax.dynamic_index_in_dim(owners, prompt_slot, 0, keepdims=False)
    start_row = device % PSPLIT * rows_here
    positions = start_row + jnp.arange(rows_here, dtype=jnp.int32)
    entries = latent_rows(kv_new, positions, latent_gain)
    entries = jnp.where((positions < length_here)[:, None], entries, 0.0).astype(jnp.bfloat16)
    layout = entries.reshape(rows_here // members, members, row_width)
    rotated = jnp.roll(layout, owner_here, axis=1)
    outgoing = rotated.transpose(1, 0, 2)
    arrived = lax.all_to_all(outgoing, "heads", split_axis=0, concat_axis=0, tiled=True)
    new_cache = arrived.reshape(members // PSPLIT, PSPLIT * (rows_here // members), row_width)
    own_keys = latent_rows(kv_dec, context_len, latent_gain).astype(jnp.bfloat16)
    own_latent = own_keys[:, :lat_width].astype(jnp.float32)
    query_latent = jnp.dot(
        query_nope[:, 0], key_absorb[0], preferred_element_type=jnp.float32
    ).astype(jnp.bfloat16)
    query_own = jnp.concatenate([query_latent, query_rope[:, 0]], axis=-1)
    query_all = lax.all_gather(query_own[:, None], "heads", axis=1, tiled=True)
    score_scale = 1.0 / math.sqrt(query_nope.shape[-1] + query_rope.shape[-1])
    position = jnp.arange(cache.shape[1], dtype=jnp.int32) * members + device
    is_live = (position[None, :] < context_len[:, None])[:, None, :]
    scores = (
        jnp.einsum("rhk,rik->rhi", query_all, cache, preferred_element_type=jnp.float32)
        * score_scale
    )
    scores = jnp.where(is_live, scores, -1e30)
    block_max = jnp.max(scores, axis=-1)
    weights = jnp.where(is_live, jnp.exp(scores - block_max[..., None]), 0.0)
    block_total = jnp.sum(weights, axis=-1)
    partial_value = jnp.einsum(
        "rhi,ril->rhl",
        weights.astype(jnp.bfloat16),
        cache[..., :lat_width],
        preferred_element_type=jnp.float32,
    )
    got_partial, got_max, got_total = (
        lax.all_to_all(partial_value[None], "heads", split_axis=2, concat_axis=0, tiled=True),
        lax.all_to_all(block_max[None], "heads", split_axis=2, concat_axis=0, tiled=True),
        lax.all_to_all(block_total[None], "heads", split_axis=2, concat_axis=0, tiled=True),
    )
    got_partial = got_partial[:, :, 0]
    got_max = got_max[:, :, 0]
    got_total = got_total[:, :, 0]
    own_score = (
        jnp.sum(query_own.astype(jnp.float32) * own_keys.astype(jnp.float32), axis=-1) * score_scale
    )
    ceiling = jnp.maximum(jnp.max(got_max, axis=0), own_score)
    factor = jnp.exp(got_max - ceiling[None])
    gathered = jnp.sum(factor[..., None] * got_partial, axis=0)
    summed = jnp.sum(factor * got_total, axis=0)
    own_weight = jnp.exp(own_score - ceiling)
    summed = summed + own_weight
    gathered = gathered + own_weight[:, None] * own_latent
    latent_out = (gathered / summed[:, None]).astype(jnp.bfloat16)
    head_out = jnp.dot(latent_out, value_absorb[0], preferred_element_type=jnp.float32).astype(
        jnp.bfloat16
    )
    head_term = jnp.dot(head_out, out_weight, preferred_element_type=jnp.float32)
    attn_out = lax.psum(head_term, "heads").astype(jnp.bfloat16)
    return (new_cache, attn_out)


MESH = pl.DeviceIdType.MESH
RING_A = 144
RING_C = 160


def fused_body(
    plen, own, clen, w_ref, gain_ref, dh_ref, qn_ref, qr_ref, ka_ref, va_ref, tab_ref, dtab_ref,
    hid_hbm, ow_hbm, cache_hbm,
    new_ref, attn_ref,
    wbuf, hb, ow, cb, acc, qbuf, kvs, kvr, msg, got, hp, rs, agp, ag, ent,
    loc, ring_s, core_s, x_s, in_r, core_r,
    q_s, q_r, qc_s, qc_r, kv_s, kv_r, a_s, a_r, rs_s, rs_r, ag_s, ag_r, n_s, n_r,
):
    me = lax.axis_index("heads")
    g = lax.axis_index("groups")
    k = me // 2
    c = me % 2
    z = k // 2
    y = k % 2
    pos = y * (7 - 2 * z) + z
    rows = w_ref.shape[0]
    width = w_ref.shape[1]
    lat = gain_ref.shape[1]
    scale = 1.0 / math.sqrt(qn_ref.shape[1] + qr_ref.shape[1])
    f32, bf16 = jnp.float32, jnp.bfloat16

    def chip(p):
        q = (p + 16) % 8
        hi = q // 4
        return hi * (15 - 2 * q) + (1 - hi) * 2 * q

    def heads(d):
        return {"heads": d}

    sib = me + 1 - 2 * c
    right = chip(pos + 1) * 2 + c
    left = chip(pos - 1) * 2 + c

    local_copies = [
        pltpu.make_async_copy(hid_hbm, hb, loc.at[0]),
        pltpu.make_async_copy(ow_hbm, ow, loc.at[1]),
        pltpu.make_async_copy(cache_hbm, cb, loc.at[2]),
        pltpu.make_async_copy(w_ref, wbuf.at[k, pl.ds(pl.multiple_of(c * rows, 16), rows)], loc.at[3]),
    ]
    for cp in (local_copies[3], local_copies[2], local_copies[0], local_copies[1]):
        cp.start()

    barrier = pltpu.get_barrier_semaphore()

    def greet(i, carry):
        pl.semaphore_signal(barrier, inc=1, device_id=heads((me + i) % 16), device_id_type=MESH)
        return carry

    lax.fori_loop(1, 16, greet, 0)
    pl.semaphore_signal(barrier, inc=1, device_id={"groups": 1 - g}, device_id_type=MESH)

    starts = (304 * g, RING_A, 304 * (1 - g))
    sizes = (RING_A, RING_C, RING_A)

    def piece(kk, cc, role):
        return wbuf.at[kk, pl.ds(pl.multiple_of(cc * rows + starts[role], 16), sizes[role])]

    def w_piece(role):
        return w_ref.at[pl.ds(pl.multiple_of(starts[role], 16), sizes[role])]

    sends = []

    def send(src, dst, ssem, rsem, dev):
        cp = pltpu.make_async_remote_copy(
            src_ref=src, dst_ref=dst, send_sem=ssem, recv_sem=rsem, device_id=dev, device_id_type=MESH
        )
        cp.start()
        sends.append(cp)

    def arrived(dst, rsem):
        pltpu.make_async_copy(dst, dst, rsem).wait()

    def q_copy(i):
        dest = ((k + i) % 8) * 2 + c
        return pltpu.make_async_remote_copy(
            src_ref=qbuf.at[c, k], dst_ref=qbuf.at[c, k], send_sem=q_s.at[i], recv_sem=q_r.at[i],
            device_id=heads(dest), device_id_type=MESH,
        )

    qlat = jnp.dot(qn_ref[...], ka_ref[...], preferred_element_type=f32).astype(bf16).astype(f32)
    q_own = jnp.concatenate([qlat, qr_ref[...].astype(f32)], axis=-1)
    qbuf[c, k] = q_own
    wide = dh_ref[:, pl.ds(pl.multiple_of(k * 2 * rows, 128), 2 * rows)].astype(f32)
    part = jnp.where(c == 0, wide[:, :rows], wide[:, rows:]).astype(bf16)
    kvs[0] = jnp.dot(part, w_ref[...], preferred_element_type=f32)

    pl.semaphore_wait(barrier, 16)

    lax.fori_loop(1, 8, lambda i, t: (q_copy(i).start(), t)[1], 0)

    def kv_send(step):
        b = 1 << step
        dest = me + b - 2 * b * ((me // b) % 2)
        send(kvs.at[step], kvr.at[step], kv_s.at[step], kv_r.at[step], heads(dest))

    def kv_take(step):
        arrived(kvr.at[step], kv_r.at[step])
        kvs[step + 1] = kvs[step] + kvr[step]

    kv_send(0)
    for role in range(2):
        mine = piece(k, c, role)
        send(w_piece(role), mine, ring_s.at[0, k, role], in_r.at[k, role], heads(right))
        send(w_piece(role), mine, ring_s.at[1, k, role], in_r.at[k, role], heads(left))
    for role in range(3):
        send(w_piece(role), piece(k, c, role), core_s.at[k, role], core_r.at[k, role], heads(sib))

    def to_core(kk, role):
        p = piece(kk, c, role)
        send(p, p, core_s.at[kk, role], core_r.at[kk, role], heads(sib))

    def ring(s, role):
        for way in range(2):
            if s == 4 and role != way:
                continue
            kk = chip(pos - s) if way == 0 else chip(pos + s)
            p = piece(kk, c, role)
            arrived(p, in_r.at[kk, role])
            if s < 3 or (s == 3 and role == way):
                send(p, p, ring_s.at[way, kk, role], in_r.at[kk, role], heads(right if way == 0 else left))
            if role == 0:
                send(p, p, x_s.at[kk], in_r.at[kk, 2], {"groups": 1 - g})
            to_core(kk, role)

    def cross(s):
        for kk in (chip(pos - s), chip(pos + s)) if s < 4 else (chip(pos + 4),):
            arrived(piece(kk, c, 2), in_r.at[kk, 2])
            to_core(kk, 2)

    def matmul(kk, first=False):
        for role in range(3):
            arrived(piece(kk, 1 - c, role), core_r.at[kk, role])
        h = hb[:, pl.ds(pl.multiple_of(kk * 2 * rows, 128), 2 * rows)]
        v = jnp.dot(h, wbuf[kk], preferred_element_type=f32)
        acc[...] = v if first else acc[...] + v

    def finish(kv, table):
        a = kv[:, :lat]
        b = kv[:, lat:]
        half = b.shape[1] // 2
        a = a * lax.rsqrt(jnp.mean(a * a, axis=-1, keepdims=True) + 1e-06) * gain_ref[...]
        turned = jnp.concatenate([b[:, half:], b[:, :half]], axis=-1)
        b = b * table[:, : 2 * half] + turned * table[:, 2 * half :]
        return jnp.concatenate([a, b], axis=-1)

    lax.fori_loop(1, 8, lambda i, t: (q_copy(i).wait_recv(), t)[1], 0)
    send(qbuf.at[c], qbuf.at[c], qc_s, qc_r, heads(sib))
    kv_take(0)
    kv_send(1)
    local_copies[2].wait()
    arrived(qbuf.at[1 - c], qc_r)

    n_req = cb.shape[0]
    per = cb.shape[1]
    cols = n_req * per
    q_all = qbuf[...].reshape(16 * n_req, width).astype(bf16)
    cache = cb[...].reshape(cols, width)
    scores = lax.dot_general(q_all, cache, (((1,), (1,)), ((), ())), preferred_element_type=f32) * scale
    row_i = lax.broadcasted_iota(jnp.int32, scores.shape, 0)
    col_i = lax.broadcasted_iota(jnp.int32, scores.shape, 1)
    limit = jnp.zeros(scores.shape, jnp.int32)
    for r in range(n_req):
        limit = jnp.where(row_i % n_req == r, clen[r], limit)
    live = (col_i // per == row_i % n_req) & ((col_i % per) * 16 + me < limit)
    scores = jnp.where(live, scores, -1e30)
    top = jnp.max(scores, axis=-1, keepdims=True)
    wts = jnp.where(live, jnp.exp(scores - top), 0.0)
    tot = jnp.sum(wts, axis=-1, keepdims=True)
    pv = jnp.dot(wts.astype(bf16), cache[:, :lat], preferred_element_type=f32)
    lane = lax.broadcasted_iota(jnp.int32, (16 * n_req, 128), 1)
    stat = jnp.where(lane == 0, top, jnp.where(lane == 1, tot, 0.0))
    msg[...] = jnp.concatenate([pv, stat], axis=-1).reshape(2, 8, n_req, lat + 128)

    def a_copy(i):
        dest = (me + i) % 16
        return pltpu.make_async_remote_copy(
            src_ref=msg.at[dest % 2, dest // 2], dst_ref=got.at[me], send_sem=a_s.at[i], recv_sem=a_r.at[i],
            device_id=heads(dest), device_id_type=MESH,
        )

    lax.fori_loop(1, 16, lambda i, t: (a_copy(i).start(), t)[1], 0)
    got[me] = msg[c, k]

    ring(1, 0)
    kv_take(1)
    kv_send(2)
    ring(1, 1)
    kv_take(2)
    kv_send(3)
    ring(2, 0)
    kv_take(3)
    own_key = finish(kvs[4], dtab_ref[...]).astype(bf16).astype(f32)
    own_score = jnp.sum(q_own * own_key, axis=-1, keepdims=True) * scale

    def from_a(i, t):
        arrived(got.at[(me + 16 - i) % 16], a_r.at[i])
        return t

    lax.fori_loop(1, 16, from_a, 0)
    gmax = got[:, :, lat : lat + 1]
    gtot = got[:, :, lat + 1 : lat + 2]
    ceiling = jnp.maximum(jnp.max(gmax, axis=0), own_score)
    fac = jnp.exp(gmax - ceiling[None])
    own_w = jnp.exp(own_score - ceiling)
    summed = jnp.sum(fac * gtot, axis=0) + own_w
    gath = jnp.sum(fac * got[:, :, :lat], axis=0) + own_w * own_key[:, :lat]
    lat_out = (gath / summed).astype(bf16)
    head_out = jnp.dot(lat_out, va_ref[...], preferred_element_type=f32).astype(bf16)
    local_copies[1].wait()
    hp[...] = jnp.dot(head_out, ow[...], preferred_element_type=f32)

    def span(d):
        return pl.ds(pl.multiple_of((d // 2) * 896 + (d % 2) * 384, 128), 512)

    def rs_copy(i):
        dest = (me + i) % 16
        return pltpu.make_async_remote_copy(
            src_ref=hp.at[:, span(dest)], dst_ref=rs.at[me], send_sem=rs_s.at[i], recv_sem=rs_r.at[i],
            device_id=heads(dest), device_id_type=MESH,
        )

    lax.fori_loop(1, 16, lambda i, t: (rs_copy(i).start(), t)[1], 0)
    rs[me] = hp[:, span(me)]
    ring(2, 1)
    cross(1)

    def from_rs(i, t):
        arrived(rs.at[(me + 16 - i) % 16], rs_r.at[i])
        return t

    lax.fori_loop(1, 16, from_rs, 0)
    total = jnp.sum(rs[...], axis=0)
    packed = jnp.concatenate([total[:, :256], total[:, 256:]], axis=0).astype(bf16)
    agp[...] = packed
    ag[me] = packed

    def ag_copy(i):
        dest = (me + i) % 16
        return pltpu.make_async_remote_copy(
            src_ref=agp, dst_ref=ag.at[me], send_sem=ag_s.at[i], recv_sem=ag_r.at[i],
            device_id=heads(dest), device_id_type=MESH,
        )

    lax.fori_loop(1, 16, lambda i, t: (ag_copy(i).start(), t)[1], 0)
    ring(3, 0)
    cross(2)
    local_copies[0].wait()
    local_copies[3].wait()
    matmul(k, True)
    ring(3, 1)
    matmul(chip(pos - 1))
    matmul(chip(pos + 1))

    def from_ag(i, t):
        arrived(ag.at[(me + 16 - i) % 16], ag_r.at[i])
        return t

    lax.fori_loop(1, 16, from_ag, 0)
    for kk in range(8):
        lo = ag[2 * kk].astype(f32)
        hi = ag[2 * kk + 1].astype(f32)
        attn_ref[:, kk * 896 : kk * 896 + 256] = lo[:8].astype(bf16)
        attn_ref[:, kk * 896 + 256 : kk * 896 + 512] = lo[8:].astype(bf16)
        attn_ref[:, kk * 896 + 512 : kk * 896 + 640] = hi[:8, 128:].astype(bf16)
        attn_ref[:, kk * 896 + 640 : kk * 896 + 896] = hi[8:].astype(bf16)
    matmul(chip(pos - 2))
    matmul(chip(pos + 2))
    ring(4, 0)
    ring(4, 1)
    cross(3)
    matmul(chip(pos - 3))
    matmul(chip(pos + 3))
    cross(4)
    matmul(chip(pos + 4))

    slot = me // 8
    m = hb.shape[0]
    position = (me % 8) * m + lax.broadcasted_iota(jnp.int32, (m, 1), 0)
    e = jnp.where(position < plen[slot], finish(acc[...], tab_ref[...]), 0.0).astype(bf16)
    o_i = lax.broadcasted_iota(jnp.int32, (m, m), 0)
    s_i = lax.broadcasted_iota(jnp.int32, (m, m), 1)
    turn = (o_i // 16 - own[slot] + 16) % 16
    perm = jnp.where(s_i == (o_i % 16) * 16 + turn, 1.0, 0.0).astype(bf16)
    ent[...] = jnp.dot(perm, e, preferred_element_type=f32).astype(bf16).reshape(ent.shape)

    def dst_of(src):
        return new_ref.at[src // 8, pl.ds(pl.multiple_of((src % 8) * 16, 16), 16)]

    def n_copy(i):
        dest = (me + i) % 16
        return pltpu.make_async_remote_copy(
            src_ref=ent.at[dest], dst_ref=dst_of(me), send_sem=n_s.at[i], recv_sem=n_r.at[i],
            device_id=heads(dest), device_id_type=MESH,
        )

    lax.fori_loop(1, 16, lambda i, t: (n_copy(i).start(), t)[1], 0)
    new_ref[slot, pl.ds(pl.multiple_of((me % 8) * 16, 16), 16)] = ent[me]
    for cp in sends:
        cp.wait_send()
    lax.fori_loop(1, 8, lambda i, t: (q_copy(i).wait_send(), t)[1], 0)

    def drain(i, t):
        a_copy(i).wait_send()
        rs_copy(i).wait_send()
        ag_copy(i).wait_send()
        return t

    lax.fori_loop(1, 16, drain, 0)

    def from_n(i, t):
        arrived(dst_of((me + 16 - i) % 16), n_r.at[i])
        n_copy(i).wait_send()
        return t

    lax.fori_loop(1, 16, from_n, 0)


def rope_table(positions, half):
    frequency = jnp.exp(jnp.arange(half, dtype=jnp.float32) * (-math.log(10000.0) / half))
    angles = positions.astype(jnp.float32)[:, None] * frequency
    co, si = jnp.cos(angles), jnp.sin(angles)
    return jnp.concatenate([co, co, -si, si], axis=-1)


def fused(
    prompt_hidden, prompt_len, owners, down_weight, latent_gain, decode_hidden, context_len,
    query_nope, query_rope, key_absorb, value_absorb, out_weight, cache,
):
    device = lax.axis_index("heads")
    m, model = prompt_hidden.shape
    rows, width = down_weight.shape
    lat = latent_gain.shape[0]
    half = (width - lat) // 2
    n_req = decode_hidden.shape[0]
    per_prompt = 16 // prompt_len.shape[0]
    positions = (device % per_prompt) * m + jnp.arange(m, dtype=jnp.int32)
    table = rope_table(positions, half)
    dtable = rope_table(context_len, half)
    f32, bf16 = jnp.float32, jnp.bfloat16
    vmem = pl.BlockSpec(memory_space=pltpu.VMEM)
    smem = pl.BlockSpec(memory_space=pltpu.SMEM)
    hbm = pl.BlockSpec(memory_space=pl.ANY)
    dma = pltpu.SemaphoreType.DMA
    return pl.pallas_call(
        fused_body,
        out_shape=(
            jax.ShapeDtypeStruct((prompt_len.shape[0], m * per_prompt // 16, width), bf16),
            jax.ShapeDtypeStruct((n_req, model), bf16),
        ),
        in_specs=[smem] * 3 + [vmem] * 9 + [hbm] * 3,
        out_specs=(vmem, vmem),
        scratch_shapes=[
            pltpu.VMEM((8, 2 * rows, width), bf16),
            pltpu.VMEM((m, model), bf16),
            pltpu.VMEM(out_weight.shape, bf16),
            pltpu.VMEM(cache.shape, bf16),
            pltpu.VMEM((m, width), f32),
            pltpu.VMEM((2, 8, n_req, width), f32),
            pltpu.VMEM((5, n_req, width), f32),
            pltpu.VMEM((4, n_req, width), f32),
            pltpu.VMEM((2, 8, n_req, lat + 128), f32),
            pltpu.VMEM((16, n_req, lat + 128), f32),
            pltpu.VMEM((n_req, model), f32),
            pltpu.VMEM((16, n_req, 512), f32),
            pltpu.VMEM((16, 256), bf16),
            pltpu.VMEM((16, 16, 256), bf16),
            pltpu.VMEM((16, m // 16, width), bf16),
            dma((4,)),
            dma((2, 8, 2)),
            dma((8, 3)),
            dma((8,)),
            dma((8, 3)),
            dma((8, 3)),
            dma((8,)), dma((8,)), dma, dma, dma((4,)), dma((4,)),
            dma((16,)), dma((16,)), dma((16,)), dma((16,)), dma((16,)), dma((16,)), dma((16,)), dma((16,)),
        ],
        compiler_params=pltpu.CompilerParams(
            collective_id=0, has_side_effects=True, vmem_limit_bytes=44 * 1024 * 1024
        ),
        cost_estimate=pl.CostEstimate(
            flops=2 * m * model * width, bytes_accessed=2 * (m * model + model * width), transcendentals=0
        ),
    )(
        prompt_len, owners, context_len, down_weight, latent_gain[None], decode_hidden, query_nope[:, 0],
        query_rope[:, 0], key_absorb[0], value_absorb[0], table, dtable, prompt_hidden, out_weight, cache,
    )


def solution(mesh):
    placed = (
        P(("groups", "heads"), None),
        P("groups"),
        P("groups"),
        P("heads", None),
        P(),
        P("groups", None),
        P("groups"),
        P("groups", "heads", None),
        P("groups", "heads", None),
        P("heads", None, None),
        P("heads", None, None),
        P("heads", None),
        P("groups", "heads", None),
    )
    small = mesh.shape["heads"] == 16 and mesh.shape["groups"] == 2
    return jax.shard_map(
        fused if small else local,
        mesh=mesh,
        in_specs=placed,
        out_specs=(P("groups", "heads", None), P("groups", None)),
        check_vma=False,
    )
```

```python
import math

import jax
import jax.numpy as jnp
from jax import lax
from jax.experimental import pallas as pl
from jax.experimental.pallas import tpu as pltpu
from jax.sharding import PartitionSpec as P

PSPLIT = 8


def latent_rows(kv_rows, positions, gain_vec):
    row_width = gain_vec.shape[0]
    latent = kv_rows[..., :row_width]
    rotary = kv_rows[..., row_width:]
    latent = (
        latent * lax.rsqrt(jnp.mean(latent * latent, axis=-1, keepdims=True) + 1e-06) * gain_vec
    )
    half_rope = rotary.shape[-1] // 2
    frequency = jnp.exp(jnp.arange(half_rope, dtype=jnp.float32) * (-math.log(10000.0) / half_rope))
    angles = positions.astype(jnp.float32)[..., None] * frequency
    cosine = jnp.cos(angles)
    sine_part = jnp.sin(angles)
    leading = rotary[..., :half_rope]
    second = rotary[..., half_rope:]
    turned = jnp.concatenate(
        [leading * cosine - second * sine_part, second * cosine + leading * sine_part], axis=-1
    )
    return jnp.concatenate([latent, turned], axis=-1)


def local(
    prompt_hidden,
    prompt_len,
    owners,
    down_weight,
    latent_gain,
    decode_hidden,
    context_len,
    query_nope,
    query_rope,
    key_absorb,
    value_absorb,
    out_weight,
    cache,
):
    members = lax.axis_size("heads")
    device = lax.axis_index("heads")
    rows_here, model_width = prompt_hidden.shape
    row_width = down_weight.shape[1]
    lat_width = latent_gain.shape[0]
    shard_rows = lax.all_gather(down_weight, "heads", axis=0, tiled=True)
    kv_new = jnp.dot(prompt_hidden, shard_rows, preferred_element_type=jnp.float32)
    kv_dec = jnp.dot(decode_hidden, shard_rows, preferred_element_type=jnp.float32)
    prompt_slot = device // PSPLIT
    length_here = lax.dynamic_index_in_dim(prompt_len, prompt_slot, 0, keepdims=False)
    owner_here = lax.dynamic_index_in_dim(owners, prompt_slot, 0, keepdims=False)
    start_row = device % PSPLIT * rows_here
    positions = start_row + jnp.arange(rows_here, dtype=jnp.int32)
    entries = latent_rows(kv_new, positions, latent_gain)
    entries = jnp.where((positions < length_here)[:, None], entries, 0.0).astype(jnp.bfloat16)
    layout = entries.reshape(rows_here // members, members, row_width)
    rotated = jnp.roll(layout, owner_here, axis=1)
    outgoing = rotated.transpose(1, 0, 2)
    arrived = lax.all_to_all(outgoing, "heads", split_axis=0, concat_axis=0, tiled=True)
    new_cache = arrived.reshape(members // PSPLIT, PSPLIT * (rows_here // members), row_width)
    own_keys = latent_rows(kv_dec, context_len, latent_gain).astype(jnp.bfloat16)
    own_latent = own_keys[:, :lat_width].astype(jnp.float32)
    query_latent = jnp.dot(
        query_nope[:, 0], key_absorb[0], preferred_element_type=jnp.float32
    ).astype(jnp.bfloat16)
    query_own = jnp.concatenate([query_latent, query_rope[:, 0]], axis=-1)
    query_all = lax.all_gather(query_own[:, None], "heads", axis=1, tiled=True)
    score_scale = 1.0 / math.sqrt(query_nope.shape[-1] + query_rope.shape[-1])
    position = jnp.arange(cache.shape[1], dtype=jnp.int32) * members + device
    is_live = (position[None, :] < context_len[:, None])[:, None, :]
    scores = (
        jnp.einsum("rhk,rik->rhi", query_all, cache, preferred_element_type=jnp.float32)
        * score_scale
    )
    scores = jnp.where(is_live, scores, -1e30)
    block_max = jnp.max(scores, axis=-1)
    weights = jnp.where(is_live, jnp.exp(scores - block_max[..., None]), 0.0)
    block_total = jnp.sum(weights, axis=-1)
    partial_value = jnp.einsum(
        "rhi,ril->rhl",
        weights.astype(jnp.bfloat16),
        cache[..., :lat_width],
        preferred_element_type=jnp.float32,
    )
    got_partial, got_max, got_total = (
        lax.all_to_all(partial_value[None], "heads", split_axis=2, concat_axis=0, tiled=True),
        lax.all_to_all(block_max[None], "heads", split_axis=2, concat_axis=0, tiled=True),
        lax.all_to_all(block_total[None], "heads", split_axis=2, concat_axis=0, tiled=True),
    )
    got_partial = got_partial[:, :, 0]
    got_max = got_max[:, :, 0]
    got_total = got_total[:, :, 0]
    own_score = (
        jnp.sum(query_own.astype(jnp.float32) * own_keys.astype(jnp.float32), axis=-1) * score_scale
    )
    ceiling = jnp.maximum(jnp.max(got_max, axis=0), own_score)
    factor = jnp.exp(got_max - ceiling[None])
    gathered = jnp.sum(factor[..., None] * got_partial, axis=0)
    summed = jnp.sum(factor * got_total, axis=0)
    own_weight = jnp.exp(own_score - ceiling)
    summed = summed + own_weight
    gathered = gathered + own_weight[:, None] * own_latent
    latent_out = (gathered / summed[:, None]).astype(jnp.bfloat16)
    head_out = jnp.dot(latent_out, value_absorb[0], preferred_element_type=jnp.float32).astype(
        jnp.bfloat16
    )
    head_term = jnp.dot(head_out, out_weight, preferred_element_type=jnp.float32)
    attn_out = lax.psum(head_term, "heads").astype(jnp.bfloat16)
    return (new_cache, attn_out)


MESH = pl.DeviceIdType.MESH
RING_A = 144
RING_C = 160


def fused_body(
    plen_h, own_h, clen_h, w_h, gain_h, dh_h, qn_h, qr_h, ka_h, va_h,
    hid_hbm, ow_hbm, cache_hbm,
    new_ref, attn_ref,
    plen, own, clen, w_ref, gain_ref, dh_ref, qn_ref, qr_ref, ka_ref, va_ref, tab_ref,
    wbuf, hb, ow, cb, acc, qbuf, kvs, kvr, msg, got, smsg, sgot, hp, rs, agp, ag, ent,
    loc, ring_s, core_s, x_s, in_r, core_r,
    q_s, q_r, qc_s, qc_r, kv_s, kv_r, a_s, a_r, s_s, s_r, rs_s, rs_r, ag_s, ag_r, n_s, n_r,
):
    me = lax.axis_index("heads")
    g = lax.axis_index("groups")
    k = me // 2
    c = me % 2
    z = k // 2
    y = k % 2
    pos = y * (7 - 2 * z) + z
    rows = w_ref.shape[0]
    width = w_ref.shape[1]
    lat = gain_ref.shape[1]
    scale = 1.0 / math.sqrt(qn_ref.shape[1] + qr_ref.shape[1])
    f32, bf16 = jnp.float32, jnp.bfloat16

    def chip(p):
        q = (p + 16) % 8
        hi = q // 4
        return hi * (15 - 2 * q) + (1 - hi) * 2 * q

    def heads(d):
        return {"heads": d}

    sib = me + 1 - 2 * c
    right = chip(pos + 1) * 2 + c
    left = chip(pos - 1) * 2 + c

    local_copies = [
        pltpu.make_async_copy(hid_hbm, hb, loc.at[0]),
        pltpu.make_async_copy(ow_hbm, ow, loc.at[1]),
        pltpu.make_async_copy(cache_hbm, cb, loc.at[2]),
        pltpu.make_async_copy(w_h, wbuf.at[k, pl.ds(pl.multiple_of(c * rows, 16), rows)], loc.at[3]),
    ]
    early = [
        pltpu.make_async_copy(src, dst, loc.at[4 + n])
        for n, (src, dst) in enumerate((
            (ka_h, ka_ref), (qn_h, qn_ref), (qr_h, qr_ref), (dh_h, dh_ref), (w_h, w_ref), (clen_h, clen),
            (gain_h, gain_ref), (va_h, va_ref), (plen_h, plen), (own_h, own),
        ))
    ]
    for cp in early + [local_copies[2], local_copies[3], local_copies[1], local_copies[0]]:
        cp.start()

    barrier = pltpu.get_barrier_semaphore()

    def greet(i, carry):
        pl.semaphore_signal(barrier, inc=1, device_id=heads((me + i) % 16), device_id_type=MESH)
        return carry

    lax.fori_loop(1, 16, greet, 0)
    pl.semaphore_signal(barrier, inc=1, device_id={"groups": 1 - g}, device_id_type=MESH)

    starts = (304 * g, RING_A, 304 * (1 - g), 304 * (1 - g), 304 * (1 - g) + 80)
    sizes = (RING_A, RING_C, RING_A, 80, 64)

    def piece(kk, cc, role):
        return wbuf.at[kk, pl.ds(pl.multiple_of(cc * rows + starts[role], 16), sizes[role])]

    def w_piece(role):
        return w_h.at[pl.ds(pl.multiple_of(starts[role], 16), sizes[role])]

    sends = []

    def send(src, dst, ssem, rsem, dev):
        cp = pltpu.make_async_remote_copy(
            src_ref=src, dst_ref=dst, send_sem=ssem, recv_sem=rsem, device_id=dev, device_id_type=MESH
        )
        cp.start()
        sends.append(cp)

    def arrived(dst, rsem):
        pltpu.make_async_copy(dst, dst, rsem).wait()

    def q_copy(i):
        dest = ((k + i) % 8) * 2 + c
        return pltpu.make_async_remote_copy(
            src_ref=qbuf.at[c, k], dst_ref=qbuf.at[c, k], send_sem=q_s.at[i], recv_sem=q_r.at[i],
            device_id=heads(dest), device_id_type=MESH,
        )

    pl.semaphore_wait(barrier, 16)
    for role in range(2):
        mine = piece(k, c, role)
        send(w_piece(role), mine, ring_s.at[0, k, role], in_r.at[k, role], heads(right))
        send(w_piece(role), mine, ring_s.at[1, k, role], in_r.at[k, role], heads(left))
    for role in range(3):
        send(w_piece(role), piece(k, c, role), core_s.at[k, role], core_r.at[k, role], heads(sib))


    for cp in early:
        cp.wait()
    qlat = jnp.dot(qn_ref[...], ka_ref[...], preferred_element_type=f32).astype(bf16).astype(f32)
    q_own = jnp.concatenate([qlat, qr_ref[...].astype(f32)], axis=-1)
    qbuf[c, k] = q_own
    wide = dh_ref[:, pl.ds(pl.multiple_of(k * 2 * rows, 128), 2 * rows)].astype(f32)
    part = jnp.where(c == 0, wide[:, :rows], wide[:, rows:]).astype(bf16)
    kvs[0] = jnp.dot(part, w_ref[...], preferred_element_type=f32)

    lax.fori_loop(1, 8, lambda i, t: (q_copy(i).start(), t)[1], 0)

    def kv_send(step):
        b = 1 << step
        dest = me + b - 2 * b * ((me // b) % 2)
        send(kvs.at[step], kvr.at[step], kv_s.at[step], kv_r.at[step], heads(dest))

    def kv_take(step):
        arrived(kvr.at[step], kv_r.at[step])
        kvs[step + 1] = kvs[step] + kvr[step]

    kv_send(0)
    def to_core(kk, role):
        p = piece(kk, c, role)
        send(p, p, core_s.at[kk, role], core_r.at[kk, role], heads(sib))

    def ring(s, role):
        for way in range(2):
            if s == 4 and role != way:
                continue
            kk = chip(pos - s) if way == 0 else chip(pos + s)
            p = piece(kk, c, role)
            arrived(p, in_r.at[kk, role])
            if s < 3 or (s == 3 and role == way):
                send(p, p, ring_s.at[way, kk, role], in_r.at[kk, role], heads(right if way == 0 else left))
            if role == 0 and s < 4:
                send(p, p, x_s.at[kk], in_r.at[kk, 2], {"groups": 1 - g})
            to_core(kk, role)

    def cross(s):
        for way in range(2):
            kk = chip(pos - s) if way == 0 else chip(pos + s)
            arrived(piece(kk, c, 2), in_r.at[kk, 2])
            if s == 3:
                p = piece(kk, c, 3 + way)
                send(p, p, ring_s.at[way, kk, 2], in_r.at[kk, 3 + way], heads(right if way == 0 else left))
            to_core(kk, 2)

    def far():
        kk = chip(pos + 4)
        for role in (3, 4):
            arrived(piece(kk, c, role), in_r.at[kk, role])
            to_core(kk, role)

    def matmul(kk, first=False, last=False):
        for role in (0, 1, 3, 4) if last else (0, 1, 2):
            arrived(piece(kk, 1 - c, role), core_r.at[kk, role])
        h = hb[:, pl.ds(pl.multiple_of(kk * 2 * rows, 128), 2 * rows)]
        v = jnp.dot(h, wbuf[kk], preferred_element_type=f32)
        acc[...] = v if first else acc[...] + v

    def finish(kv, table):
        a = kv[:, :lat]
        b = kv[:, lat:]
        half = b.shape[1] // 2
        a = a * lax.rsqrt(jnp.mean(a * a, axis=-1, keepdims=True) + 1e-06) * gain_ref[...]
        turned = jnp.concatenate([b[:, half:], b[:, :half]], axis=-1)
        b = b * table[:, : 2 * half] + turned * table[:, 2 * half :]
        return jnp.concatenate([a, b], axis=-1)

    lax.fori_loop(1, 8, lambda i, t: (q_copy(i).wait_recv(), t)[1], 0)
    send(qbuf.at[c], qbuf.at[c], qc_s, qc_r, heads(sib))
    ring(1, 0)
    kv_take(0)
    kv_send(1)
    local_copies[2].wait()
    arrived(qbuf.at[1 - c], qc_r)

    n_req = cb.shape[0]
    per = cb.shape[1]
    cols = n_req * per
    q_all = qbuf[...].reshape(16 * n_req, width).astype(bf16)
    cache = cb[...].reshape(cols, width)
    scores = lax.dot_general(q_all, cache, (((1,), (1,)), ((), ())), preferred_element_type=f32) * scale
    row_i = lax.broadcasted_iota(jnp.int32, scores.shape, 0)
    col_i = lax.broadcasted_iota(jnp.int32, scores.shape, 1)
    limit = jnp.zeros(scores.shape, jnp.int32)
    for r in range(n_req):
        limit = jnp.where(row_i % n_req == r, clen[r], limit)
    live = (col_i // per == row_i % n_req) & ((col_i % per) * 16 + me < limit)
    scores = jnp.where(live, scores, -1e30)
    top = jnp.max(scores, axis=-1, keepdims=True)
    wts = jnp.where(live, jnp.exp(scores - top), 0.0)
    tot = jnp.sum(wts, axis=-1, keepdims=True)
    pv = jnp.dot(wts.astype(bf16), cache[:, :lat], preferred_element_type=f32)
    lane = lax.broadcasted_iota(jnp.int32, (16 * n_req, 128), 1)
    stat = jnp.where(lane == 0, top, jnp.where(lane == 1, tot, 0.0))
    pv = pv.reshape(16, n_req, lat)
    msg[...] = jnp.concatenate([pv[:, :, : lat // 2], pv[:, :, lat // 2 :]], axis=1).astype(bf16)
    smsg[...] = stat.reshape(16, n_req, 128)

    def a_copy(i):
        dest = (me + i) % 16
        return pltpu.make_async_remote_copy(
            src_ref=msg.at[(dest % 2) * 8 + dest // 2], dst_ref=got.at[me], send_sem=a_s.at[i], recv_sem=a_r.at[i],
            device_id=heads(dest), device_id_type=MESH,
        )

    def s_copy(i):
        dest = (me + i) % 16
        return pltpu.make_async_remote_copy(
            src_ref=smsg.at[(dest % 2) * 8 + dest // 2], dst_ref=sgot.at[me], send_sem=s_s.at[i], recv_sem=s_r.at[i],
            device_id=heads(dest), device_id_type=MESH,
        )

    lax.fori_loop(1, 16, lambda i, t: (a_copy(i).start(), s_copy(i).start(), t)[2], 0)
    got[me] = msg[c * 8 + k]
    sgot[me] = smsg[c * 8 + k]

    slot = me // 8
    m = hb.shape[0]
    position = (me % 8) * m + lax.broadcasted_iota(jnp.int32, (m, 1), 0)
    half = (width - lat) // 2
    tab_ref[...] = rope_table(position, half)
    req = lax.broadcasted_iota(jnp.int32, (n_req, 1), 0)
    dpos = jnp.zeros((n_req, 1), jnp.int32)
    for r in range(n_req):
        dpos = jnp.where(req == r, clen[r], dpos)
    dtab = rope_table(dpos, half)
    kv_take(1)
    kv_send(2)
    ring(1, 1)
    kv_take(2)
    kv_send(3)
    ring(2, 0)
    kv_take(3)
    own_key = finish(kvs[4], dtab).astype(bf16).astype(f32)
    own_score = jnp.sum(q_own * own_key, axis=-1, keepdims=True) * scale

    def from_a(i, t):
        arrived(got.at[(me + 16 - i) % 16], a_r.at[i])
        arrived(sgot.at[(me + 16 - i) % 16], s_r.at[i])
        return t

    lax.fori_loop(1, 16, from_a, 0)
    gmax = sgot[:, :, 0:1]
    gtot = sgot[:, :, 1:2]
    ceiling = jnp.maximum(jnp.max(gmax, axis=0), own_score)
    fac = jnp.exp(gmax - ceiling[None])
    own_w = jnp.exp(own_score - ceiling)
    summed = jnp.sum(fac * gtot, axis=0) + own_w
    both = jnp.sum(jnp.concatenate([fac, fac], axis=1) * got[...].astype(f32), axis=0)
    gath = jnp.concatenate([both[:n_req], both[n_req:]], axis=1) + own_w * own_key[:, :lat]
    lat_out = (gath / summed).astype(bf16)
    head_out = jnp.dot(lat_out, va_ref[...], preferred_element_type=f32).astype(bf16)
    local_copies[1].wait()
    flat = jnp.dot(head_out, ow[...], preferred_element_type=f32)
    for d in range(16):
        lo = (d // 2) * 896 + (d % 2) * 384
        hp[d] = jnp.concatenate([flat[:, lo : lo + 256], flat[:, lo + 256 : lo + 512]], axis=0).astype(bf16)

    def rs_copy(i):
        dest = (me + i) % 16
        return pltpu.make_async_remote_copy(
            src_ref=hp.at[dest], dst_ref=rs.at[me], send_sem=rs_s.at[i], recv_sem=rs_r.at[i],
            device_id=heads(dest), device_id_type=MESH,
        )

    lax.fori_loop(1, 16, lambda i, t: (rs_copy(i).start(), t)[1], 0)
    rs[me] = hp[me]
    ring(2, 1)
    cross(1)
    ring(3, 0)

    def from_rs(i, t):
        arrived(rs.at[(me + 16 - i) % 16], rs_r.at[i])
        return t

    lax.fori_loop(1, 16, from_rs, 0)
    packed = jnp.sum(rs[...].astype(f32), axis=0).astype(bf16)
    agp[...] = packed
    ag[me] = packed

    def ag_copy(i):
        dest = (me + i) % 16
        return pltpu.make_async_remote_copy(
            src_ref=agp, dst_ref=ag.at[me], send_sem=ag_s.at[i], recv_sem=ag_r.at[i],
            device_id=heads(dest), device_id_type=MESH,
        )

    lax.fori_loop(1, 16, lambda i, t: (ag_copy(i).start(), t)[1], 0)
    cross(2)
    local_copies[0].wait()
    local_copies[3].wait()
    matmul(k, True)
    ring(3, 1)
    matmul(chip(pos - 1))
    matmul(chip(pos + 1))

    def from_ag(i, t):
        arrived(ag.at[(me + 16 - i) % 16], ag_r.at[i])
        return t

    lax.fori_loop(1, 16, from_ag, 0)
    for kk in range(8):
        lo = ag[2 * kk].astype(f32)
        hi = ag[2 * kk + 1].astype(f32)
        attn_ref[:, kk * 896 : kk * 896 + 256] = lo[:8].astype(bf16)
        attn_ref[:, kk * 896 + 256 : kk * 896 + 512] = lo[8:].astype(bf16)
        attn_ref[:, kk * 896 + 512 : kk * 896 + 640] = hi[:8, 128:].astype(bf16)
        attn_ref[:, kk * 896 + 640 : kk * 896 + 896] = hi[8:].astype(bf16)
    matmul(chip(pos - 2))
    matmul(chip(pos + 2))
    cross(3)
    ring(4, 0)
    ring(4, 1)
    matmul(chip(pos - 3))
    matmul(chip(pos + 3))
    far()
    matmul(chip(pos + 4), last=True)

    e = jnp.where(position < plen[slot], finish(acc[...], tab_ref[...]), 0.0).astype(bf16)
    o_i = lax.broadcasted_iota(jnp.int32, (m, m), 0)
    s_i = lax.broadcasted_iota(jnp.int32, (m, m), 1)
    turn = (o_i // 16 - own[slot] + 16) % 16
    perm = jnp.where(s_i == (o_i % 16) * 16 + turn, 1.0, 0.0).astype(bf16)
    ent[...] = jnp.dot(perm, e, preferred_element_type=f32).astype(bf16).reshape(ent.shape)

    def dst_of(src):
        return new_ref.at[src // 8, pl.ds(pl.multiple_of((src % 8) * 16, 16), 16)]

    def n_copy(i):
        dest = (me + i) % 16
        return pltpu.make_async_remote_copy(
            src_ref=ent.at[dest], dst_ref=dst_of(me), send_sem=n_s.at[i], recv_sem=n_r.at[i],
            device_id=heads(dest), device_id_type=MESH,
        )

    lax.fori_loop(1, 16, lambda i, t: (n_copy(i).start(), t)[1], 0)
    new_ref[slot, pl.ds(pl.multiple_of((me % 8) * 16, 16), 16)] = ent[me]
    for cp in sends:
        cp.wait_send()
    lax.fori_loop(1, 8, lambda i, t: (q_copy(i).wait_send(), t)[1], 0)

    def drain(i, t):
        a_copy(i).wait_send()
        s_copy(i).wait_send()
        rs_copy(i).wait_send()
        ag_copy(i).wait_send()
        return t

    lax.fori_loop(1, 16, drain, 0)

    def from_n(i, t):
        arrived(dst_of((me + 16 - i) % 16), n_r.at[i])
        n_copy(i).wait_send()
        return t

    lax.fori_loop(1, 16, from_n, 0)


def rope_table(positions, half):
    lane = lax.broadcasted_iota(jnp.int32, (positions.shape[0], 4 * half), 1)
    index = (lane % half).astype(jnp.float32)
    angles = positions.astype(jnp.float32) * jnp.exp(index * (-math.log(10000.0) / half))
    sine = jnp.where(lane < 3 * half, -jnp.sin(angles), jnp.sin(angles))
    return jnp.where(lane < 2 * half, jnp.cos(angles), sine)


def fused(
    prompt_hidden, prompt_len, owners, down_weight, latent_gain, decode_hidden, context_len,
    query_nope, query_rope, key_absorb, value_absorb, out_weight, cache,
):
    m, model = prompt_hidden.shape
    rows, width = down_weight.shape
    lat = latent_gain.shape[0]
    n_req = decode_hidden.shape[0]
    per_prompt = 16 // prompt_len.shape[0]
    f32, bf16 = jnp.float32, jnp.bfloat16
    small = (
        prompt_len, owners, context_len, down_weight, latent_gain[None], decode_hidden, query_nope[:, 0],
        query_rope[:, 0], key_absorb[0], value_absorb[0],
    )
    vmem = pl.BlockSpec(memory_space=pltpu.VMEM)
    hbm = pl.BlockSpec(memory_space=pltpu.HBM)
    dma = pltpu.SemaphoreType.DMA
    return pl.pallas_call(
        fused_body,
        out_shape=(
            jax.ShapeDtypeStruct((prompt_len.shape[0], m * per_prompt // 16, width), bf16),
            jax.ShapeDtypeStruct((n_req, model), bf16),
        ),
        in_specs=[hbm] * (len(small) + 3),
        out_specs=(vmem, vmem),
        scratch_shapes=[pltpu.SMEM(a.shape, a.dtype) for a in small[:3]]
        + [pltpu.VMEM(a.shape, a.dtype) for a in small[3:]]
        + [
            pltpu.VMEM((m, 2 * (width - lat)), f32),
            pltpu.VMEM((8, 2 * rows, width), bf16),
            pltpu.VMEM((m, model), bf16),
            pltpu.VMEM(out_weight.shape, bf16),
            pltpu.VMEM(cache.shape, bf16),
            pltpu.VMEM((m, width), f32),
            pltpu.VMEM((2, 8, n_req, width), f32),
            pltpu.VMEM((5, n_req, width), f32),
            pltpu.VMEM((4, n_req, width), f32),
            pltpu.VMEM((16, 2 * n_req, lat // 2), bf16),
            pltpu.VMEM((16, 2 * n_req, lat // 2), bf16),
            pltpu.VMEM((16, n_req, 128), f32),
            pltpu.VMEM((16, n_req, 128), f32),
            pltpu.VMEM((16, 16, 256), bf16),
            pltpu.VMEM((16, 16, 256), bf16),
            pltpu.VMEM((16, 256), bf16),
            pltpu.VMEM((16, 16, 256), bf16),
            pltpu.VMEM((16, m // 16, width), bf16),
            dma((16,)),
            dma((2, 8, 3)),
            dma((8, 5)),
            dma((8,)),
            dma((8, 5)),
            dma((8, 5)),
            dma((8,)), dma((8,)), dma, dma, dma((4,)), dma((4,)),
            dma((16,)), dma((16,)), dma((16,)), dma((16,)), dma((16,)), dma((16,)), dma((16,)), dma((16,)), dma((16,)), dma((16,)),
        ],
        compiler_params=pltpu.CompilerParams(
            collective_id=0, has_side_effects=True, vmem_limit_bytes=60 * 1024 * 1024
        ),
        cost_estimate=pl.CostEstimate(
            flops=2 * m * model * width, bytes_accessed=2 * (m * model + model * width), transcendentals=0
        ),
    )(*small, prompt_hidden, out_weight, cache)


def solution(mesh):
    placed = (
        P(("groups", "heads"), None),
        P("groups"),
        P("groups"),
        P("heads", None),
        P(),
        P("groups", None),
        P("groups"),
        P("groups", "heads", None),
        P("groups", "heads", None),
        P("heads", None, None),
        P("heads", None, None),
        P("heads", None),
        P("groups", "heads", None),
    )
    small = mesh.shape["heads"] == 16 and mesh.shape["groups"] == 2
    return jax.shard_map(
        fused if small else local,
        mesh=mesh,
        in_specs=placed,
        out_specs=(P("groups", "heads", None), P("groups", None)),
        check_vma=False,
    )
```

```python
import math

import jax
import jax.numpy as jnp
from jax import lax
from jax.experimental import pallas as pl
from jax.experimental.pallas import tpu as pltpu
from jax.sharding import PartitionSpec as P

PSPLIT = 8


def latent_rows(kv_rows, positions, gain_vec):
    row_width = gain_vec.shape[0]
    latent = kv_rows[..., :row_width]
    rotary = kv_rows[..., row_width:]
    latent = (
        latent * lax.rsqrt(jnp.mean(latent * latent, axis=-1, keepdims=True) + 1e-06) * gain_vec
    )
    half_rope = rotary.shape[-1] // 2
    frequency = jnp.exp(jnp.arange(half_rope, dtype=jnp.float32) * (-math.log(10000.0) / half_rope))
    angles = positions.astype(jnp.float32)[..., None] * frequency
    cosine = jnp.cos(angles)
    sine_part = jnp.sin(angles)
    leading = rotary[..., :half_rope]
    second = rotary[..., half_rope:]
    turned = jnp.concatenate(
        [leading * cosine - second * sine_part, second * cosine + leading * sine_part], axis=-1
    )
    return jnp.concatenate([latent, turned], axis=-1)


def local(
    prompt_hidden,
    prompt_len,
    owners,
    down_weight,
    latent_gain,
    decode_hidden,
    context_len,
    query_nope,
    query_rope,
    key_absorb,
    value_absorb,
    out_weight,
    cache,
):
    members = lax.axis_size("heads")
    device = lax.axis_index("heads")
    rows_here, model_width = prompt_hidden.shape
    row_width = down_weight.shape[1]
    lat_width = latent_gain.shape[0]
    shard_rows = lax.all_gather(down_weight, "heads", axis=0, tiled=True)
    kv_new = jnp.dot(prompt_hidden, shard_rows, preferred_element_type=jnp.float32)
    kv_dec = jnp.dot(decode_hidden, shard_rows, preferred_element_type=jnp.float32)
    prompt_slot = device // PSPLIT
    length_here = lax.dynamic_index_in_dim(prompt_len, prompt_slot, 0, keepdims=False)
    owner_here = lax.dynamic_index_in_dim(owners, prompt_slot, 0, keepdims=False)
    start_row = device % PSPLIT * rows_here
    positions = start_row + jnp.arange(rows_here, dtype=jnp.int32)
    entries = latent_rows(kv_new, positions, latent_gain)
    entries = jnp.where((positions < length_here)[:, None], entries, 0.0).astype(jnp.bfloat16)
    layout = entries.reshape(rows_here // members, members, row_width)
    rotated = jnp.roll(layout, owner_here, axis=1)
    outgoing = rotated.transpose(1, 0, 2)
    arrived = lax.all_to_all(outgoing, "heads", split_axis=0, concat_axis=0, tiled=True)
    new_cache = arrived.reshape(members // PSPLIT, PSPLIT * (rows_here // members), row_width)
    own_keys = latent_rows(kv_dec, context_len, latent_gain).astype(jnp.bfloat16)
    own_latent = own_keys[:, :lat_width].astype(jnp.float32)
    query_latent = jnp.dot(
        query_nope[:, 0], key_absorb[0], preferred_element_type=jnp.float32
    ).astype(jnp.bfloat16)
    query_own = jnp.concatenate([query_latent, query_rope[:, 0]], axis=-1)
    query_all = lax.all_gather(query_own[:, None], "heads", axis=1, tiled=True)
    score_scale = 1.0 / math.sqrt(query_nope.shape[-1] + query_rope.shape[-1])
    position = jnp.arange(cache.shape[1], dtype=jnp.int32) * members + device
    is_live = (position[None, :] < context_len[:, None])[:, None, :]
    scores = (
        jnp.einsum("rhk,rik->rhi", query_all, cache, preferred_element_type=jnp.float32)
        * score_scale
    )
    scores = jnp.where(is_live, scores, -1e30)
    block_max = jnp.max(scores, axis=-1)
    weights = jnp.where(is_live, jnp.exp(scores - block_max[..., None]), 0.0)
    block_total = jnp.sum(weights, axis=-1)
    partial_value = jnp.einsum(
        "rhi,ril->rhl",
        weights.astype(jnp.bfloat16),
        cache[..., :lat_width],
        preferred_element_type=jnp.float32,
    )
    got_partial, got_max, got_total = (
        lax.all_to_all(partial_value[None], "heads", split_axis=2, concat_axis=0, tiled=True),
        lax.all_to_all(block_max[None], "heads", split_axis=2, concat_axis=0, tiled=True),
        lax.all_to_all(block_total[None], "heads", split_axis=2, concat_axis=0, tiled=True),
    )
    got_partial = got_partial[:, :, 0]
    got_max = got_max[:, :, 0]
    got_total = got_total[:, :, 0]
    own_score = (
        jnp.sum(query_own.astype(jnp.float32) * own_keys.astype(jnp.float32), axis=-1) * score_scale
    )
    ceiling = jnp.maximum(jnp.max(got_max, axis=0), own_score)
    factor = jnp.exp(got_max - ceiling[None])
    gathered = jnp.sum(factor[..., None] * got_partial, axis=0)
    summed = jnp.sum(factor * got_total, axis=0)
    own_weight = jnp.exp(own_score - ceiling)
    summed = summed + own_weight
    gathered = gathered + own_weight[:, None] * own_latent
    latent_out = (gathered / summed[:, None]).astype(jnp.bfloat16)
    head_out = jnp.dot(latent_out, value_absorb[0], preferred_element_type=jnp.float32).astype(
        jnp.bfloat16
    )
    head_term = jnp.dot(head_out, out_weight, preferred_element_type=jnp.float32)
    attn_out = lax.psum(head_term, "heads").astype(jnp.bfloat16)
    return (new_cache, attn_out)


MESH = pl.DeviceIdType.MESH
RING_A = 176
RING_C = 96
RING = RING_A + RING_C
FAR = 48


def fused_body(
    plen_h, own_h, clen_h, w_h, gain_h, dh_h, qn_h, qr_h, ka_h, va_h,
    hid_hbm, ow_hbm, cache_hbm,
    new_ref, attn_ref,
    plen, own, clen, w_ref, gain_ref, dh_ref, qn_ref, qr_ref, ka_ref, va_ref, tab_ref,
    wbuf, hb, ow, cb, acc, qbuf, kvs, kvr, msg, got, smsg, sgot, hp, rs, agp, ag, ent,
    loc, ring_s, core_s, x_s, in_r, core_r,
    q_s, q_r, qc_s, qc_r, agc_s, agc_r, kv_s, kv_r, a_s, a_r, s_s, s_r, rs_s, rs_r, ag_s, ag_r, n_s, n_r,
):
    me = lax.axis_index("heads")
    g = lax.axis_index("groups")
    k = me // 2
    c = me % 2
    z = k // 2
    y = k % 2
    pos = y * (7 - 2 * z) + z
    rows = w_ref.shape[0]
    width = w_ref.shape[1]
    lat = gain_ref.shape[1]
    scale = 1.0 / math.sqrt(qn_ref.shape[1] + qr_ref.shape[1])
    f32, bf16 = jnp.float32, jnp.bfloat16

    def chip(p):
        q = (p + 16) % 8
        hi = q // 4
        return hi * (15 - 2 * q) + (1 - hi) * 2 * q

    def heads(d):
        return {"heads": d}

    sib = me + 1 - 2 * c
    right = chip(pos + 1) * 2 + c
    left = chip(pos - 1) * 2 + c

    local_copies = [
        pltpu.make_async_copy(hid_hbm, hb, loc.at[0]),
        pltpu.make_async_copy(ow_hbm, ow, loc.at[1]),
        pltpu.make_async_copy(cache_hbm, cb, loc.at[2]),
        pltpu.make_async_copy(w_h, wbuf.at[k, pl.ds(pl.multiple_of(c * rows, 16), rows)], loc.at[3]),
    ]
    early = [
        pltpu.make_async_copy(src, dst, loc.at[4 + n])
        for n, (src, dst) in enumerate((
            (ka_h, ka_ref), (qn_h, qn_ref), (qr_h, qr_ref), (dh_h, dh_ref), (w_h, w_ref), (clen_h, clen),
            (gain_h, gain_ref), (va_h, va_ref), (plen_h, plen), (own_h, own),
        ))
    ]
    for cp in early + [local_copies[2], local_copies[3], local_copies[1], local_copies[0]]:
        cp.start()

    barrier = pltpu.get_barrier_semaphore()

    def greet(i, carry):
        pl.semaphore_signal(barrier, inc=1, device_id=heads((me + i) % 16), device_id_type=MESH)
        return carry

    lax.fori_loop(1, 16, greet, 0)
    pl.semaphore_signal(barrier, inc=1, device_id={"groups": 1 - g}, device_id_type=MESH)

    starts = (RING * g, RING_A, RING * (1 - g), RING * (1 - g), RING * (1 - g) + FAR)
    sizes = (RING_A, RING_C, RING_A, FAR, RING_A - FAR)

    def piece(kk, cc, role):
        return wbuf.at[kk, pl.ds(pl.multiple_of(cc * rows + starts[role], 16), sizes[role])]

    def w_piece(role):
        return w_h.at[pl.ds(pl.multiple_of(starts[role], 16), sizes[role])]

    sends = []

    def send(src, dst, ssem, rsem, dev):
        cp = pltpu.make_async_remote_copy(
            src_ref=src, dst_ref=dst, send_sem=ssem, recv_sem=rsem, device_id=dev, device_id_type=MESH
        )
        cp.start()
        sends.append(cp)

    def arrived(dst, rsem):
        pltpu.make_async_copy(dst, dst, rsem).wait()

    def q_copy(i):
        dest = ((k + i) % 8) * 2 + c
        return pltpu.make_async_remote_copy(
            src_ref=qbuf.at[c, k], dst_ref=qbuf.at[c, k], send_sem=q_s.at[i], recv_sem=q_r.at[i],
            device_id=heads(dest), device_id_type=MESH,
        )

    pl.semaphore_wait(barrier, 16)
    for role in range(2):
        mine = piece(k, c, role)
        send(w_piece(role), mine, ring_s.at[0, k, role], in_r.at[k, role], heads(right))
        send(w_piece(role), mine, ring_s.at[1, k, role], in_r.at[k, role], heads(left))
    for role in range(3):
        send(w_piece(role), piece(k, c, role), core_s.at[k, role], core_r.at[k, role], heads(sib))


    for cp in early:
        cp.wait()
    qlat = jnp.dot(qn_ref[...], ka_ref[...], preferred_element_type=f32).astype(bf16).astype(f32)
    q_own = jnp.concatenate([qlat, qr_ref[...].astype(f32)], axis=-1)
    fold = 384
    tail = jnp.concatenate([q_own[:, fold:], jnp.zeros((q_own.shape[0], 2 * fold - width), f32)], axis=-1)
    qbuf[c, k] = jnp.concatenate([q_own[:, :fold], tail], axis=0).astype(bf16)
    wide = dh_ref[:, pl.ds(pl.multiple_of(k * 2 * rows, 128), 2 * rows)].astype(f32)
    part = jnp.where(c == 0, wide[:, :rows], wide[:, rows:]).astype(bf16)
    kvs[0] = jnp.dot(part, w_ref[...], preferred_element_type=f32)

    lax.fori_loop(1, 8, lambda i, t: (q_copy(i).start(), t)[1], 0)

    def kv_send(step):
        b = 1 << step
        dest = me + b - 2 * b * ((me // b) % 2)
        send(kvs.at[step], kvr.at[step], kv_s.at[step], kv_r.at[step], heads(dest))

    def kv_take(step):
        arrived(kvr.at[step], kv_r.at[step])
        kvs[step + 1] = kvs[step] + kvr[step]

    kv_send(0)
    def to_core(kk, role):
        p = piece(kk, c, role)
        send(p, p, core_s.at[kk, role], core_r.at[kk, role], heads(sib))

    def ring(s, role):
        for way in range(2):
            if s == 4 and role != way:
                continue
            kk = chip(pos - s) if way == 0 else chip(pos + s)
            p = piece(kk, c, role)
            arrived(p, in_r.at[kk, role])
            if s < 3 or (s == 3 and role == way):
                send(p, p, ring_s.at[way, kk, role], in_r.at[kk, role], heads(right if way == 0 else left))
            if role == 0 and s < 4:
                send(p, p, x_s.at[kk], in_r.at[kk, 2], {"groups": 1 - g})
            to_core(kk, role)

    def cross(s):
        for way in range(2):
            kk = chip(pos - s) if way == 0 else chip(pos + s)
            arrived(piece(kk, c, 2), in_r.at[kk, 2])
            if s == 3:
                p = piece(kk, c, 3 + way)
                send(p, p, ring_s.at[way, kk, 2], in_r.at[kk, 3 + way], heads(right if way == 0 else left))
            to_core(kk, 2)

    def far():
        kk = chip(pos + 4)
        for role in (3, 4):
            arrived(piece(kk, c, role), in_r.at[kk, role])
            to_core(kk, role)

    def matmul(kk, first=False, last=False):
        for role in (0, 1, 3, 4) if last else (0, 1, 2):
            arrived(piece(kk, 1 - c, role), core_r.at[kk, role])
        h = hb[:, pl.ds(pl.multiple_of(kk * 2 * rows, 128), 2 * rows)]
        v = jnp.dot(h, wbuf[kk], preferred_element_type=f32)
        acc[...] = v if first else acc[...] + v

    def finish(kv, table):
        a = kv[:, :lat]
        b = kv[:, lat:]
        half = b.shape[1] // 2
        a = a * lax.rsqrt(jnp.mean(a * a, axis=-1, keepdims=True) + 1e-06) * gain_ref[...]
        turned = jnp.concatenate([b[:, half:], b[:, :half]], axis=-1)
        b = b * table[:, : 2 * half] + turned * table[:, 2 * half :]
        return jnp.concatenate([a, b], axis=-1)

    lax.fori_loop(1, 8, lambda i, t: (q_copy(i).wait_recv(), t)[1], 0)
    send(qbuf.at[c], qbuf.at[c], qc_s, qc_r, heads(sib))
    ring(1, 0)
    kv_take(0)
    kv_send(1)
    local_copies[2].wait()
    arrived(qbuf.at[1 - c], qc_r)

    n_req = cb.shape[0]
    per = cb.shape[1]
    cols = n_req * per
    q_all = qbuf[...].astype(f32).reshape(16, 2 * n_req, fold)
    q_all = jnp.concatenate(
        [
            q_all[:, :n_req].reshape(16 * n_req, fold),
            q_all[:, n_req:].reshape(16 * n_req, fold)[:, : width - fold],
        ],
        axis=-1,
    ).astype(bf16)
    cache = cb[...].reshape(cols, width)
    scores = lax.dot_general(q_all, cache, (((1,), (1,)), ((), ())), preferred_element_type=f32) * scale
    row_i = lax.broadcasted_iota(jnp.int32, scores.shape, 0)
    col_i = lax.broadcasted_iota(jnp.int32, scores.shape, 1)
    limit = jnp.zeros(scores.shape, jnp.int32)
    for r in range(n_req):
        limit = jnp.where(row_i % n_req == r, clen[r], limit)
    live = (col_i // per == row_i % n_req) & ((col_i % per) * 16 + me < limit)
    scores = jnp.where(live, scores, -1e30)
    top = jnp.max(scores, axis=-1, keepdims=True)
    wts = jnp.where(live, jnp.exp(scores - top), 0.0)
    tot = jnp.sum(wts, axis=-1, keepdims=True)
    pv = jnp.dot(wts.astype(bf16), cache[:, :lat], preferred_element_type=f32)
    lane = lax.broadcasted_iota(jnp.int32, (16 * n_req, 128), 1)
    stat = jnp.where(lane == 0, top, jnp.where(lane == 1, tot, 0.0))
    pv = pv.reshape(16, n_req, lat)
    msg[...] = jnp.concatenate([pv[:, :, : lat // 2], pv[:, :, lat // 2 :]], axis=1).astype(bf16)
    smsg[...] = stat.reshape(16, n_req, 128)

    def a_copy(i):
        dest = (me + i) % 16
        return pltpu.make_async_remote_copy(
            src_ref=msg.at[(dest % 2) * 8 + dest // 2], dst_ref=got.at[me], send_sem=a_s.at[i], recv_sem=a_r.at[i],
            device_id=heads(dest), device_id_type=MESH,
        )

    def s_copy(i):
        dest = (me + i) % 16
        return pltpu.make_async_remote_copy(
            src_ref=smsg.at[(dest % 2) * 8 + dest // 2], dst_ref=sgot.at[me], send_sem=s_s.at[i], recv_sem=s_r.at[i],
            device_id=heads(dest), device_id_type=MESH,
        )

    lax.fori_loop(1, 16, lambda i, t: (a_copy(i).start(), s_copy(i).start(), t)[2], 0)
    got[me] = msg[c * 8 + k]
    sgot[me] = smsg[c * 8 + k]

    slot = me // 8
    m = hb.shape[0]
    position = (me % 8) * m + lax.broadcasted_iota(jnp.int32, (m, 1), 0)
    half = (width - lat) // 2
    tab_ref[...] = rope_table(position, half)
    req = lax.broadcasted_iota(jnp.int32, (n_req, 1), 0)
    dpos = jnp.zeros((n_req, 1), jnp.int32)
    for r in range(n_req):
        dpos = jnp.where(req == r, clen[r], dpos)
    dtab = rope_table(dpos, half)
    kv_take(1)
    kv_send(2)
    ring(1, 1)
    kv_take(2)
    kv_send(3)
    ring(2, 0)
    kv_take(3)
    own_key = finish(kvs[4], dtab).astype(bf16).astype(f32)
    own_score = jnp.sum(q_own * own_key, axis=-1, keepdims=True) * scale

    def from_a(i, t):
        arrived(got.at[(me + 16 - i) % 16], a_r.at[i])
        arrived(sgot.at[(me + 16 - i) % 16], s_r.at[i])
        return t

    lax.fori_loop(1, 16, from_a, 0)
    gmax = sgot[:, :, 0:1]
    gtot = sgot[:, :, 1:2]
    ceiling = jnp.maximum(jnp.max(gmax, axis=0), own_score)
    fac = jnp.exp(gmax - ceiling[None])
    own_w = jnp.exp(own_score - ceiling)
    summed = jnp.sum(fac * gtot, axis=0) + own_w
    both = jnp.sum(jnp.concatenate([fac, fac], axis=1) * got[...].astype(f32), axis=0)
    gath = jnp.concatenate([both[:n_req], both[n_req:]], axis=1) + own_w * own_key[:, :lat]
    lat_out = (gath / summed).astype(bf16)
    head_out = jnp.dot(lat_out, va_ref[...], preferred_element_type=f32).astype(bf16)
    local_copies[1].wait()
    flat = jnp.dot(head_out, ow[...], preferred_element_type=f32)
    for d in range(16):
        lo = (d // 2) * 896 + (d % 2) * 384
        hp[d] = jnp.concatenate([flat[:, lo : lo + 256], flat[:, lo + 256 : lo + 512]], axis=0).astype(bf16)

    def rs_copy(i):
        dest = (me + i) % 16
        return pltpu.make_async_remote_copy(
            src_ref=hp.at[dest], dst_ref=rs.at[me], send_sem=rs_s.at[i], recv_sem=rs_r.at[i],
            device_id=heads(dest), device_id_type=MESH,
        )

    lax.fori_loop(1, 16, lambda i, t: (rs_copy(i).start(), t)[1], 0)
    rs[me] = hp[me]
    ring(2, 1)
    cross(1)
    ring(3, 0)

    def from_rs(i, t):
        arrived(rs.at[(me + 16 - i) % 16], rs_r.at[i])
        return t

    lax.fori_loop(1, 16, from_rs, 0)
    packed = jnp.sum(rs[...].astype(f32), axis=0).astype(bf16)
    agp[...] = packed
    ag[c, k] = packed

    def ag_copy(i):
        dest = ((k + i) % 8) * 2 + c
        return pltpu.make_async_remote_copy(
            src_ref=agp, dst_ref=ag.at[c, k], send_sem=ag_s.at[i], recv_sem=ag_r.at[i],
            device_id=heads(dest), device_id_type=MESH,
        )

    lax.fori_loop(1, 8, lambda i, t: (ag_copy(i).start(), t)[1], 0)
    cross(2)
    local_copies[0].wait()
    local_copies[3].wait()
    matmul(k, True)
    ring(3, 1)
    cross(3)
    matmul(chip(pos - 1))
    matmul(chip(pos + 1))

    def from_ag(i, t):
        arrived(ag.at[c, (k + 8 - i) % 8], ag_r.at[i])
        return t

    lax.fori_loop(1, 8, from_ag, 0)
    send(ag.at[c], ag.at[c], agc_s, agc_r, heads(sib))
    matmul(chip(pos - 2))
    matmul(chip(pos + 2))
    arrived(ag.at[1 - c], agc_r)
    for kk in range(8):
        lo = ag[0, kk].astype(f32)
        hi = ag[1, kk].astype(f32)
        attn_ref[:, kk * 896 : kk * 896 + 256] = lo[:8].astype(bf16)
        attn_ref[:, kk * 896 + 256 : kk * 896 + 512] = lo[8:].astype(bf16)
        attn_ref[:, kk * 896 + 512 : kk * 896 + 640] = hi[:8, 128:].astype(bf16)
        attn_ref[:, kk * 896 + 640 : kk * 896 + 896] = hi[8:].astype(bf16)
    ring(4, 0)
    ring(4, 1)
    matmul(chip(pos - 3))
    matmul(chip(pos + 3))
    far()
    matmul(chip(pos + 4), last=True)

    e = jnp.where(position < plen[slot], finish(acc[...], tab_ref[...]), 0.0).astype(bf16)
    o_i = lax.broadcasted_iota(jnp.int32, (m, m), 0)
    s_i = lax.broadcasted_iota(jnp.int32, (m, m), 1)
    turn = (o_i // 16 - own[slot] + 16) % 16
    perm = jnp.where(s_i == (o_i % 16) * 16 + turn, 1.0, 0.0).astype(bf16)
    ent[...] = jnp.dot(perm, e, preferred_element_type=f32).astype(bf16).reshape(ent.shape)

    def dst_of(src):
        return new_ref.at[src // 8, pl.ds(pl.multiple_of((src % 8) * 16, 16), 16)]

    def n_copy(i):
        dest = (me + i) % 16
        return pltpu.make_async_remote_copy(
            src_ref=ent.at[dest], dst_ref=dst_of(me), send_sem=n_s.at[i], recv_sem=n_r.at[i],
            device_id=heads(dest), device_id_type=MESH,
        )

    lax.fori_loop(1, 16, lambda i, t: (n_copy(i).start(), t)[1], 0)
    new_ref[slot, pl.ds(pl.multiple_of((me % 8) * 16, 16), 16)] = ent[me]
    for cp in sends:
        cp.wait_send()
    lax.fori_loop(1, 8, lambda i, t: (q_copy(i).wait_send(), ag_copy(i).wait_send(), t)[2], 0)

    def drain(i, t):
        a_copy(i).wait_send()
        s_copy(i).wait_send()
        rs_copy(i).wait_send()
        return t

    lax.fori_loop(1, 16, drain, 0)

    def from_n(i, t):
        arrived(dst_of((me + 16 - i) % 16), n_r.at[i])
        n_copy(i).wait_send()
        return t

    lax.fori_loop(1, 16, from_n, 0)


def rope_table(positions, half):
    lane = lax.broadcasted_iota(jnp.int32, (positions.shape[0], 4 * half), 1)
    index = (lane % half).astype(jnp.float32)
    angles = positions.astype(jnp.float32) * jnp.exp(index * (-math.log(10000.0) / half))
    sine = jnp.where(lane < 3 * half, -jnp.sin(angles), jnp.sin(angles))
    return jnp.where(lane < 2 * half, jnp.cos(angles), sine)


def fused(
    prompt_hidden, prompt_len, owners, down_weight, latent_gain, decode_hidden, context_len,
    query_nope, query_rope, key_absorb, value_absorb, out_weight, cache,
):
    m, model = prompt_hidden.shape
    rows, width = down_weight.shape
    lat = latent_gain.shape[0]
    n_req = decode_hidden.shape[0]
    per_prompt = 16 // prompt_len.shape[0]
    f32, bf16 = jnp.float32, jnp.bfloat16
    small = (
        prompt_len, owners, context_len, down_weight, latent_gain[None], decode_hidden, query_nope[:, 0],
        query_rope[:, 0], key_absorb[0], value_absorb[0],
    )
    vmem = pl.BlockSpec(memory_space=pltpu.VMEM)
    hbm = pl.BlockSpec(memory_space=pltpu.HBM)
    dma = pltpu.SemaphoreType.DMA
    return pl.pallas_call(
        fused_body,
        out_shape=(
            jax.ShapeDtypeStruct((prompt_len.shape[0], m * per_prompt // 16, width), bf16),
            jax.ShapeDtypeStruct((n_req, model), bf16),
        ),
        in_specs=[hbm] * (len(small) + 3),
        out_specs=(vmem, vmem),
        scratch_shapes=[pltpu.SMEM(a.shape, a.dtype) for a in small[:3]]
        + [pltpu.VMEM(a.shape, a.dtype) for a in small[3:]]
        + [
            pltpu.VMEM((m, 2 * (width - lat)), f32),
            pltpu.VMEM((8, 2 * rows, width), bf16),
            pltpu.VMEM((m, model), bf16),
            pltpu.VMEM(out_weight.shape, bf16),
            pltpu.VMEM(cache.shape, bf16),
            pltpu.VMEM((m, width), f32),
            pltpu.VMEM((2, 8, 2 * n_req, 384), bf16),
            pltpu.VMEM((5, n_req, width), f32),
            pltpu.VMEM((4, n_req, width), f32),
            pltpu.VMEM((16, 2 * n_req, lat // 2), bf16),
            pltpu.VMEM((16, 2 * n_req, lat // 2), bf16),
            pltpu.VMEM((16, n_req, 128), f32),
            pltpu.VMEM((16, n_req, 128), f32),
            pltpu.VMEM((16, 16, 256), bf16),
            pltpu.VMEM((16, 16, 256), bf16),
            pltpu.VMEM((16, 256), bf16),
            pltpu.VMEM((2, 8, 16, 256), bf16),
            pltpu.VMEM((16, m // 16, width), bf16),
            dma((16,)),
            dma((2, 8, 3)),
            dma((8, 5)),
            dma((8,)),
            dma((8, 5)),
            dma((8, 5)),
            dma((8,)), dma((8,)), dma, dma, dma, dma, dma((4,)), dma((4,)),
            dma((16,)), dma((16,)), dma((16,)), dma((16,)), dma((16,)), dma((16,)), dma((16,)), dma((16,)), dma((16,)), dma((16,)),
        ],
        compiler_params=pltpu.CompilerParams(
            collective_id=0, has_side_effects=True, vmem_limit_bytes=60 * 1024 * 1024
        ),
        cost_estimate=pl.CostEstimate(
            flops=2 * m * model * width, bytes_accessed=2 * (m * model + model * width), transcendentals=0
        ),
    )(*small, prompt_hidden, out_weight, cache)


def solution(mesh):
    placed = (
        P(("groups", "heads"), None),
        P("groups"),
        P("groups"),
        P("heads", None),
        P(),
        P("groups", None),
        P("groups"),
        P("groups", "heads", None),
        P("groups", "heads", None),
        P("heads", None, None),
        P("heads", None, None),
        P("heads", None),
        P("groups", "heads", None),
    )
    small = mesh.shape["heads"] == 16 and mesh.shape["groups"] == 2
    return jax.shard_map(
        fused if small else local,
        mesh=mesh,
        in_specs=placed,
        out_specs=(P("groups", "heads", None), P("groups", None)),
        check_vma=False,
    )
```

```python
import math

import jax
import jax.numpy as jnp
from jax import lax
from jax.experimental import pallas as pl
from jax.experimental.pallas import tpu as pltpu
from jax.sharding import PartitionSpec as P

PSPLIT = 8


def latent_rows(kv_rows, positions, gain_vec):
    row_width = gain_vec.shape[0]
    latent = kv_rows[..., :row_width]
    rotary = kv_rows[..., row_width:]
    latent = (
        latent * lax.rsqrt(jnp.mean(latent * latent, axis=-1, keepdims=True) + 1e-06) * gain_vec
    )
    half_rope = rotary.shape[-1] // 2
    frequency = jnp.exp(jnp.arange(half_rope, dtype=jnp.float32) * (-math.log(10000.0) / half_rope))
    angles = positions.astype(jnp.float32)[..., None] * frequency
    cosine = jnp.cos(angles)
    sine_part = jnp.sin(angles)
    leading = rotary[..., :half_rope]
    second = rotary[..., half_rope:]
    turned = jnp.concatenate(
        [leading * cosine - second * sine_part, second * cosine + leading * sine_part], axis=-1
    )
    return jnp.concatenate([latent, turned], axis=-1)


def local(
    prompt_hidden,
    prompt_len,
    owners,
    down_weight,
    latent_gain,
    decode_hidden,
    context_len,
    query_nope,
    query_rope,
    key_absorb,
    value_absorb,
    out_weight,
    cache,
):
    members = lax.axis_size("heads")
    device = lax.axis_index("heads")
    rows_here, model_width = prompt_hidden.shape
    row_width = down_weight.shape[1]
    lat_width = latent_gain.shape[0]
    shard_rows = lax.all_gather(down_weight, "heads", axis=0, tiled=True)
    kv_new = jnp.dot(prompt_hidden, shard_rows, preferred_element_type=jnp.float32)
    kv_dec = jnp.dot(decode_hidden, shard_rows, preferred_element_type=jnp.float32)
    prompt_slot = device // PSPLIT
    length_here = lax.dynamic_index_in_dim(prompt_len, prompt_slot, 0, keepdims=False)
    owner_here = lax.dynamic_index_in_dim(owners, prompt_slot, 0, keepdims=False)
    start_row = device % PSPLIT * rows_here
    positions = start_row + jnp.arange(rows_here, dtype=jnp.int32)
    entries = latent_rows(kv_new, positions, latent_gain)
    entries = jnp.where((positions < length_here)[:, None], entries, 0.0).astype(jnp.bfloat16)
    layout = entries.reshape(rows_here // members, members, row_width)
    rotated = jnp.roll(layout, owner_here, axis=1)
    outgoing = rotated.transpose(1, 0, 2)
    arrived = lax.all_to_all(outgoing, "heads", split_axis=0, concat_axis=0, tiled=True)
    new_cache = arrived.reshape(members // PSPLIT, PSPLIT * (rows_here // members), row_width)
    own_keys = latent_rows(kv_dec, context_len, latent_gain).astype(jnp.bfloat16)
    own_latent = own_keys[:, :lat_width].astype(jnp.float32)
    query_latent = jnp.dot(
        query_nope[:, 0], key_absorb[0], preferred_element_type=jnp.float32
    ).astype(jnp.bfloat16)
    query_own = jnp.concatenate([query_latent, query_rope[:, 0]], axis=-1)
    query_all = lax.all_gather(query_own[:, None], "heads", axis=1, tiled=True)
    score_scale = 1.0 / math.sqrt(query_nope.shape[-1] + query_rope.shape[-1])
    position = jnp.arange(cache.shape[1], dtype=jnp.int32) * members + device
    is_live = (position[None, :] < context_len[:, None])[:, None, :]
    scores = (
        jnp.einsum("rhk,rik->rhi", query_all, cache, preferred_element_type=jnp.float32)
        * score_scale
    )
    scores = jnp.where(is_live, scores, -1e30)
    block_max = jnp.max(scores, axis=-1)
    weights = jnp.where(is_live, jnp.exp(scores - block_max[..., None]), 0.0)
    block_total = jnp.sum(weights, axis=-1)
    partial_value = jnp.einsum(
        "rhi,ril->rhl",
        weights.astype(jnp.bfloat16),
        cache[..., :lat_width],
        preferred_element_type=jnp.float32,
    )
    got_partial, got_max, got_total = (
        lax.all_to_all(partial_value[None], "heads", split_axis=2, concat_axis=0, tiled=True),
        lax.all_to_all(block_max[None], "heads", split_axis=2, concat_axis=0, tiled=True),
        lax.all_to_all(block_total[None], "heads", split_axis=2, concat_axis=0, tiled=True),
    )
    got_partial = got_partial[:, :, 0]
    got_max = got_max[:, :, 0]
    got_total = got_total[:, :, 0]
    own_score = (
        jnp.sum(query_own.astype(jnp.float32) * own_keys.astype(jnp.float32), axis=-1) * score_scale
    )
    ceiling = jnp.maximum(jnp.max(got_max, axis=0), own_score)
    factor = jnp.exp(got_max - ceiling[None])
    gathered = jnp.sum(factor[..., None] * got_partial, axis=0)
    summed = jnp.sum(factor * got_total, axis=0)
    own_weight = jnp.exp(own_score - ceiling)
    summed = summed + own_weight
    gathered = gathered + own_weight[:, None] * own_latent
    latent_out = (gathered / summed[:, None]).astype(jnp.bfloat16)
    head_out = jnp.dot(latent_out, value_absorb[0], preferred_element_type=jnp.float32).astype(
        jnp.bfloat16
    )
    head_term = jnp.dot(head_out, out_weight, preferred_element_type=jnp.float32)
    attn_out = lax.psum(head_term, "heads").astype(jnp.bfloat16)
    return (new_cache, attn_out)


MESH = pl.DeviceIdType.MESH
RING_A = 176
RING_C = 96
RING = RING_A + RING_C
FAR = 48


def fused_body(
    plen_h, own_h, clen_h, w_h, gain_h, dh_h, qn_h, qr_h, ka_h, va_h,
    hid_hbm, ow_hbm, cache_hbm,
    new_ref, attn_ref,
    plen, own, clen, w_ref, gain_ref, dh_ref, qn_ref, qr_ref, ka_ref, va_ref, tab_ref,
    wbuf, hb, ow, cb, acc, qbuf, kvs, kvr, msg, got, smsg, sgot, hp, rs, agp, ag, ent, perm_ref,
    loc, ring_s, core_s, x_s, in_r, core_r,
    q_s, q_r, qc_s, qc_r, agc_s, agc_r, kv_s, kv_r, a_s, a_r, s_s, s_r, rs_s, rs_r, ag_s, ag_r, n_s, n_r,
):
    me = lax.axis_index("heads")
    g = lax.axis_index("groups")
    k = me // 2
    c = me % 2
    z = k // 2
    y = k % 2
    pos = y * (7 - 2 * z) + z
    rows = w_ref.shape[0]
    width = w_ref.shape[1]
    lat = gain_ref.shape[1]
    scale = 1.0 / math.sqrt(qn_ref.shape[1] + qr_ref.shape[1])
    f32, bf16 = jnp.float32, jnp.bfloat16

    def chip(p):
        q = (p + 16) % 8
        hi = q // 4
        return hi * (15 - 2 * q) + (1 - hi) * 2 * q

    def heads(d):
        return {"heads": d}

    sib = me + 1 - 2 * c
    right = chip(pos + 1) * 2 + c
    left = chip(pos - 1) * 2 + c

    local_copies = [
        pltpu.make_async_copy(hid_hbm, hb, loc.at[0]),
        pltpu.make_async_copy(ow_hbm, ow, loc.at[1]),
        pltpu.make_async_copy(cache_hbm, cb, loc.at[2]),
        pltpu.make_async_copy(w_h, wbuf.at[k, pl.ds(pl.multiple_of(c * rows, 16), rows)], loc.at[3]),
    ]
    early = [
        pltpu.make_async_copy(src, dst, loc.at[4 + n])
        for n, (src, dst) in enumerate((
            (ka_h, ka_ref), (qn_h, qn_ref), (qr_h, qr_ref), (dh_h, dh_ref), (w_h, w_ref), (clen_h, clen),
            (gain_h, gain_ref), (va_h, va_ref), (plen_h, plen), (own_h, own),
        ))
    ]
    for cp in early + [local_copies[2], local_copies[3], local_copies[1], local_copies[0]]:
        cp.start()

    barrier = pltpu.get_barrier_semaphore()

    def greet(i, carry):
        pl.semaphore_signal(barrier, inc=1, device_id=heads((me + i) % 16), device_id_type=MESH)
        return carry

    lax.fori_loop(1, 16, greet, 0)
    pl.semaphore_signal(barrier, inc=1, device_id={"groups": 1 - g}, device_id_type=MESH)

    starts = (RING * g, RING_A, RING * (1 - g), RING * (1 - g), RING * (1 - g) + FAR)
    sizes = (RING_A, RING_C, RING_A, FAR, RING_A - FAR)

    def piece(kk, cc, role):
        return wbuf.at[kk, pl.ds(pl.multiple_of(cc * rows + starts[role], 16), sizes[role])]

    def w_piece(role):
        return w_h.at[pl.ds(pl.multiple_of(starts[role], 16), sizes[role])]

    sends = []

    def send(src, dst, ssem, rsem, dev):
        cp = pltpu.make_async_remote_copy(
            src_ref=src, dst_ref=dst, send_sem=ssem, recv_sem=rsem, device_id=dev, device_id_type=MESH
        )
        cp.start()
        sends.append(cp)

    def arrived(dst, rsem):
        pltpu.make_async_copy(dst, dst, rsem).wait()

    def q_copy(i):
        dest = ((k + i) % 8) * 2 + c
        return pltpu.make_async_remote_copy(
            src_ref=qbuf.at[c, k], dst_ref=qbuf.at[c, k], send_sem=q_s.at[i], recv_sem=q_r.at[i],
            device_id=heads(dest), device_id_type=MESH,
        )

    pl.semaphore_wait(barrier, 16)
    for role in range(2):
        mine = piece(k, c, role)
        send(w_piece(role), mine, ring_s.at[0, k, role], in_r.at[k, role], heads(right))
        send(w_piece(role), mine, ring_s.at[1, k, role], in_r.at[k, role], heads(left))
    for role in range(3):
        send(w_piece(role), piece(k, c, role), core_s.at[k, role], core_r.at[k, role], heads(sib))


    for cp in early:
        cp.wait()
    qlat = jnp.dot(qn_ref[...], ka_ref[...], preferred_element_type=f32).astype(bf16).astype(f32)
    q_own = jnp.concatenate([qlat, qr_ref[...].astype(f32)], axis=-1)
    fold = 384
    tail = jnp.concatenate([q_own[:, fold:], jnp.zeros((q_own.shape[0], 2 * fold - width), f32)], axis=-1)
    qbuf[c, k] = jnp.concatenate([q_own[:, :fold], tail], axis=0).astype(bf16)
    wide = dh_ref[:, pl.ds(pl.multiple_of(k * 2 * rows, 128), 2 * rows)].astype(f32)
    part = jnp.where(c == 0, wide[:, :rows], wide[:, rows:]).astype(bf16)
    kvs[0] = jnp.dot(part, w_ref[...], preferred_element_type=f32)

    lax.fori_loop(1, 8, lambda i, t: (q_copy(i).start(), t)[1], 0)

    def kv_send(step):
        b = 1 << step
        dest = me + b - 2 * b * ((me // b) % 2)
        send(kvs.at[step], kvr.at[step], kv_s.at[step], kv_r.at[step], heads(dest))

    def kv_take(step):
        arrived(kvr.at[step], kv_r.at[step])
        kvs[step + 1] = kvs[step] + kvr[step]

    kv_send(0)
    def to_core(kk, role):
        p = piece(kk, c, role)
        send(p, p, core_s.at[kk, role], core_r.at[kk, role], heads(sib))

    def ring(s, role):
        for way in range(2):
            if s == 4 and role != way:
                continue
            kk = chip(pos - s) if way == 0 else chip(pos + s)
            p = piece(kk, c, role)
            arrived(p, in_r.at[kk, role])
            if s < 3 or (s == 3 and role == way):
                send(p, p, ring_s.at[way, kk, role], in_r.at[kk, role], heads(right if way == 0 else left))
            if role == 0 and s < 4:
                send(p, p, x_s.at[kk], in_r.at[kk, 2], {"groups": 1 - g})
            to_core(kk, role)

    def cross(s):
        for way in range(2):
            kk = chip(pos - s) if way == 0 else chip(pos + s)
            arrived(piece(kk, c, 2), in_r.at[kk, 2])
            if s == 3:
                p = piece(kk, c, 3 + way)
                send(p, p, ring_s.at[way, kk, 2], in_r.at[kk, 3 + way], heads(right if way == 0 else left))
            to_core(kk, 2)

    def far():
        kk = chip(pos + 4)
        for role in (3, 4):
            arrived(piece(kk, c, role), in_r.at[kk, role])
            to_core(kk, role)

    def matmul(kk, first=False, last=False):
        for role in (0, 1, 3, 4) if last else (0, 1, 2):
            arrived(piece(kk, 1 - c, role), core_r.at[kk, role])
        h = hb[:, pl.ds(pl.multiple_of(kk * 2 * rows, 128), 2 * rows)]
        v = jnp.dot(h, wbuf[kk], preferred_element_type=f32)
        acc[...] = v if first else acc[...] + v

    def finish(kv, table):
        a = kv[:, :lat]
        b = kv[:, lat:]
        half = b.shape[1] // 2
        a = a * lax.rsqrt(jnp.mean(a * a, axis=-1, keepdims=True) + 1e-06) * gain_ref[...]
        turned = jnp.concatenate([b[:, half:], b[:, :half]], axis=-1)
        b = b * table[:, : 2 * half] + turned * table[:, 2 * half :]
        return jnp.concatenate([a, b], axis=-1)

    lax.fori_loop(1, 8, lambda i, t: (q_copy(i).wait_recv(), t)[1], 0)
    send(qbuf.at[c], qbuf.at[c], qc_s, qc_r, heads(sib))
    ring(1, 0)
    kv_take(0)
    kv_send(1)
    local_copies[2].wait()
    arrived(qbuf.at[1 - c], qc_r)

    n_req = cb.shape[0]
    per = cb.shape[1]
    cols = n_req * per
    q_all = qbuf[...].astype(f32).reshape(16, 2 * n_req, fold)
    q_all = jnp.concatenate(
        [
            q_all[:, :n_req].reshape(16 * n_req, fold),
            q_all[:, n_req:].reshape(16 * n_req, fold)[:, : width - fold],
        ],
        axis=-1,
    ).astype(bf16)
    cache = cb[...].reshape(cols, width)
    scores = lax.dot_general(q_all, cache, (((1,), (1,)), ((), ())), preferred_element_type=f32) * scale
    row_i = lax.broadcasted_iota(jnp.int32, scores.shape, 0)
    col_i = lax.broadcasted_iota(jnp.int32, scores.shape, 1)
    limit = jnp.zeros(scores.shape, jnp.int32)
    for r in range(n_req):
        limit = jnp.where(row_i % n_req == r, clen[r], limit)
    live = (col_i // per == row_i % n_req) & ((col_i % per) * 16 + me < limit)
    scores = jnp.where(live, scores, -1e30)
    top = jnp.max(scores, axis=-1, keepdims=True)
    wts = jnp.where(live, jnp.exp(scores - top), 0.0)
    tot = jnp.sum(wts, axis=-1, keepdims=True)
    pv = jnp.dot(wts.astype(bf16), cache[:, :lat], preferred_element_type=f32)
    lane = lax.broadcasted_iota(jnp.int32, (16 * n_req, 128), 1)
    stat = jnp.where(lane == 0, top, jnp.where(lane == 1, tot, 0.0))
    pv = pv.reshape(16, n_req, lat)
    msg[...] = jnp.concatenate([pv[:, :, : lat // 2], pv[:, :, lat // 2 :]], axis=1).astype(bf16)
    smsg[...] = stat.reshape(16, n_req, 128)

    def a_copy(i):
        dest = (me + i) % 16
        return pltpu.make_async_remote_copy(
            src_ref=msg.at[(dest % 2) * 8 + dest // 2], dst_ref=got.at[me], send_sem=a_s.at[i], recv_sem=a_r.at[i],
            device_id=heads(dest), device_id_type=MESH,
        )

    def s_copy(i):
        dest = (me + i) % 16
        return pltpu.make_async_remote_copy(
            src_ref=smsg.at[(dest % 2) * 8 + dest // 2], dst_ref=sgot.at[me], send_sem=s_s.at[i], recv_sem=s_r.at[i],
            device_id=heads(dest), device_id_type=MESH,
        )

    lax.fori_loop(1, 16, lambda i, t: (a_copy(i).start(), s_copy(i).start(), t)[2], 0)
    got[me] = msg[c * 8 + k]
    sgot[me] = smsg[c * 8 + k]

    slot = me // 8
    m = hb.shape[0]
    position = (me % 8) * m + lax.broadcasted_iota(jnp.int32, (m, 1), 0)
    half = (width - lat) // 2
    tab_ref[...] = rope_table(position, half)
    req = lax.broadcasted_iota(jnp.int32, (n_req, 1), 0)
    dpos = jnp.zeros((n_req, 1), jnp.int32)
    for r in range(n_req):
        dpos = jnp.where(req == r, clen[r], dpos)
    dtab = rope_table(dpos, half)
    kv_take(1)
    kv_send(2)
    ring(1, 1)
    kv_take(2)
    kv_send(3)
    ring(2, 0)
    kv_take(3)
    own_key = finish(kvs[4], dtab).astype(bf16).astype(f32)
    own_score = jnp.sum(q_own * own_key, axis=-1, keepdims=True) * scale

    def from_a(i, t):
        arrived(got.at[(me + 16 - i) % 16], a_r.at[i])
        arrived(sgot.at[(me + 16 - i) % 16], s_r.at[i])
        return t

    lax.fori_loop(1, 16, from_a, 0)
    gmax = sgot[:, :, 0:1]
    gtot = sgot[:, :, 1:2]
    ceiling = jnp.maximum(jnp.max(gmax, axis=0), own_score)
    fac = jnp.exp(gmax - ceiling[None])
    own_w = jnp.exp(own_score - ceiling)
    summed = jnp.sum(fac * gtot, axis=0) + own_w
    both = jnp.sum(jnp.concatenate([fac, fac], axis=1) * got[...].astype(f32), axis=0)
    gath = jnp.concatenate([both[:n_req], both[n_req:]], axis=1) + own_w * own_key[:, :lat]
    lat_out = (gath / summed).astype(bf16)
    head_out = jnp.dot(lat_out, va_ref[...], preferred_element_type=f32).astype(bf16)
    local_copies[1].wait()
    flat = jnp.dot(head_out, ow[...], preferred_element_type=f32)
    for d in range(16):
        lo = (d // 2) * 896 + (d % 2) * 384
        hp[d] = jnp.concatenate([flat[:, lo : lo + 256], flat[:, lo + 256 : lo + 512]], axis=0).astype(bf16)

    def rs_copy(i):
        dest = (me + i) % 16
        return pltpu.make_async_remote_copy(
            src_ref=hp.at[dest], dst_ref=rs.at[me], send_sem=rs_s.at[i], recv_sem=rs_r.at[i],
            device_id=heads(dest), device_id_type=MESH,
        )

    lax.fori_loop(1, 16, lambda i, t: (rs_copy(i).start(), t)[1], 0)
    rs[me] = hp[me]
    ring(2, 1)
    cross(1)
    ring(3, 0)

    def from_rs(i, t):
        arrived(rs.at[(me + 16 - i) % 16], rs_r.at[i])
        return t

    lax.fori_loop(1, 16, from_rs, 0)
    packed = jnp.sum(rs[...].astype(f32), axis=0).astype(bf16)
    agp[...] = packed
    ag[c, k] = packed

    def ag_copy(i):
        dest = ((k + i) % 8) * 2 + c
        return pltpu.make_async_remote_copy(
            src_ref=agp, dst_ref=ag.at[c, k], send_sem=ag_s.at[i], recv_sem=ag_r.at[i],
            device_id=heads(dest), device_id_type=MESH,
        )

    lax.fori_loop(1, 8, lambda i, t: (ag_copy(i).start(), t)[1], 0)
    cross(2)
    local_copies[0].wait()
    local_copies[3].wait()
    matmul(k, True)
    ring(3, 1)
    cross(3)
    matmul(chip(pos - 1))
    matmul(chip(pos + 1))

    def from_ag(i, t):
        arrived(ag.at[c, (k + 8 - i) % 8], ag_r.at[i])
        return t

    lax.fori_loop(1, 8, from_ag, 0)
    send(ag.at[c], ag.at[c], agc_s, agc_r, heads(sib))
    matmul(chip(pos - 2))
    matmul(chip(pos + 2))
    arrived(ag.at[1 - c], agc_r)
    for kk in range(8):
        lo = ag[0, kk].astype(f32)
        hi = ag[1, kk].astype(f32)
        attn_ref[:, kk * 896 : kk * 896 + 256] = lo[:8].astype(bf16)
        attn_ref[:, kk * 896 + 256 : kk * 896 + 512] = lo[8:].astype(bf16)
        attn_ref[:, kk * 896 + 512 : kk * 896 + 640] = hi[:8, 128:].astype(bf16)
        attn_ref[:, kk * 896 + 640 : kk * 896 + 896] = hi[8:].astype(bf16)
    ring(4, 0)
    ring(4, 1)
    matmul(chip(pos - 3))
    matmul(chip(pos + 3))
    o_i = lax.broadcasted_iota(jnp.int32, (m, m), 0)
    s_i = lax.broadcasted_iota(jnp.int32, (m, m), 1)
    turn = (o_i // 16 - own[slot] + 16) % 16
    perm_ref[...] = jnp.where(s_i == (o_i % 16) * 16 + turn, 1.0, 0.0).astype(bf16)
    far()
    matmul(chip(pos + 4), last=True)

    e = jnp.where(position < plen[slot], finish(acc[...], tab_ref[...]), 0.0).astype(bf16)
    ent[...] = jnp.dot(perm_ref[...], e, preferred_element_type=f32).astype(bf16).reshape(ent.shape)

    def dst_of(src):
        return new_ref.at[src // 8, pl.ds(pl.multiple_of((src % 8) * 16, 16), 16)]

    def n_copy(i):
        dest = (me + i) % 16
        return pltpu.make_async_remote_copy(
            src_ref=ent.at[dest], dst_ref=dst_of(me), send_sem=n_s.at[i], recv_sem=n_r.at[i],
            device_id=heads(dest), device_id_type=MESH,
        )

    lax.fori_loop(1, 16, lambda i, t: (n_copy(i).start(), t)[1], 0)
    new_ref[slot, pl.ds(pl.multiple_of((me % 8) * 16, 16), 16)] = ent[me]
    for cp in sends:
        cp.wait_send()
    lax.fori_loop(1, 8, lambda i, t: (q_copy(i).wait_send(), ag_copy(i).wait_send(), t)[2], 0)

    def drain(i, t):
        a_copy(i).wait_send()
        s_copy(i).wait_send()
        rs_copy(i).wait_send()
        return t

    lax.fori_loop(1, 16, drain, 0)

    def from_n(i, t):
        arrived(dst_of((me + 16 - i) % 16), n_r.at[i])
        n_copy(i).wait_send()
        return t

    lax.fori_loop(1, 16, from_n, 0)


def rope_table(positions, half):
    lane = lax.broadcasted_iota(jnp.int32, (positions.shape[0], 4 * half), 1)
    index = (lane % half).astype(jnp.float32)
    angles = positions.astype(jnp.float32) * jnp.exp(index * (-math.log(10000.0) / half))
    sine = jnp.where(lane < 3 * half, -jnp.sin(angles), jnp.sin(angles))
    return jnp.where(lane < 2 * half, jnp.cos(angles), sine)


def fused(
    prompt_hidden, prompt_len, owners, down_weight, latent_gain, decode_hidden, context_len,
    query_nope, query_rope, key_absorb, value_absorb, out_weight, cache,
):
    m, model = prompt_hidden.shape
    rows, width = down_weight.shape
    lat = latent_gain.shape[0]
    n_req = decode_hidden.shape[0]
    per_prompt = 16 // prompt_len.shape[0]
    f32, bf16 = jnp.float32, jnp.bfloat16
    small = (
        prompt_len, owners, context_len, down_weight, latent_gain[None], decode_hidden, query_nope[:, 0],
        query_rope[:, 0], key_absorb[0], value_absorb[0],
    )
    vmem = pl.BlockSpec(memory_space=pltpu.VMEM)
    hbm = pl.BlockSpec(memory_space=pltpu.HBM)
    dma = pltpu.SemaphoreType.DMA
    return pl.pallas_call(
        fused_body,
        out_shape=(
            jax.ShapeDtypeStruct((prompt_len.shape[0], m * per_prompt // 16, width), bf16),
            jax.ShapeDtypeStruct((n_req, model), bf16),
        ),
        in_specs=[hbm] * (len(small) + 3),
        out_specs=(vmem, vmem),
        scratch_shapes=[pltpu.SMEM(a.shape, a.dtype) for a in small[:3]]
        + [pltpu.VMEM(a.shape, a.dtype) for a in small[3:]]
        + [
            pltpu.VMEM((m, 2 * (width - lat)), f32),
            pltpu.VMEM((8, 2 * rows, width), bf16),
            pltpu.VMEM((m, model), bf16),
            pltpu.VMEM(out_weight.shape, bf16),
            pltpu.VMEM(cache.shape, bf16),
            pltpu.VMEM((m, width), f32),
            pltpu.VMEM((2, 8, 2 * n_req, 384), bf16),
            pltpu.VMEM((5, n_req, width), f32),
            pltpu.VMEM((4, n_req, width), f32),
            pltpu.VMEM((16, 2 * n_req, lat // 2), bf16),
            pltpu.VMEM((16, 2 * n_req, lat // 2), bf16),
            pltpu.VMEM((16, n_req, 128), f32),
            pltpu.VMEM((16, n_req, 128), f32),
            pltpu.VMEM((16, 16, 256), bf16),
            pltpu.VMEM((16, 16, 256), bf16),
            pltpu.VMEM((16, 256), bf16),
            pltpu.VMEM((2, 8, 16, 256), bf16),
            pltpu.VMEM((16, m // 16, width), bf16),
            pltpu.VMEM((m, m), bf16),
            dma((16,)),
            dma((2, 8, 3)),
            dma((8, 5)),
            dma((8,)),
            dma((8, 5)),
            dma((8, 5)),
            dma((8,)), dma((8,)), dma, dma, dma, dma, dma((4,)), dma((4,)),
            dma((16,)), dma((16,)), dma((16,)), dma((16,)), dma((16,)), dma((16,)), dma((16,)), dma((16,)), dma((16,)), dma((16,)),
        ],
        compiler_params=pltpu.CompilerParams(
            collective_id=0, has_side_effects=True, vmem_limit_bytes=60 * 1024 * 1024
        ),
        cost_estimate=pl.CostEstimate(
            flops=2 * m * model * width, bytes_accessed=2 * (m * model + model * width), transcendentals=0
        ),
    )(*small, prompt_hidden, out_weight, cache)


def solution(mesh):
    placed = (
        P(("groups", "heads"), None),
        P("groups"),
        P("groups"),
        P("heads", None),
        P(),
        P("groups", None),
        P("groups"),
        P("groups", "heads", None),
        P("groups", "heads", None),
        P("heads", None, None),
        P("heads", None, None),
        P("heads", None),
        P("groups", "heads", None),
    )
    small = mesh.shape["heads"] == 16 and mesh.shape["groups"] == 2
    return jax.shard_map(
        fused if small else local,
        mesh=mesh,
        in_specs=placed,
        out_specs=(P("groups", "heads", None), P("groups", None)),
        check_vma=False,
    )
```
